512 devices in a mesh: rows: 128 (over z, x, core), batch: 4 (over y).
Axes of the slice: x: 4, y: 4, z: 16, core: 2. Of those that a mesh axis runs over, the one named last changes fastest.
Arguments:
- pixels: float32 [48, 256, 512], P('batch', 'rows'), parts along dimension 0, may hold values from -8 to 8
- probes: int32 [48, 256, 512], P('batch', 'rows'), parts along dimension 0, may hold values from 0 to 1
- in_weight: bfloat16 [3, 3, 12, 512], replicated, may hold values from -0.625 to 0.625
- in_bias: float32 [512], replicated, may hold values from -3 to 3
- in_beta: float32 [512], replicated, may hold values from 0.5 to 4
- mid_weight: bfloat16 [512, 512], replicated, may hold values from -0.25 to 0.25
- mid_bias: float32 [512], replicated, may hold values from -3 to 3
- mid_beta: float32 [512], replicated, may hold values from 0.5 to 4
- out_weight: bfloat16 [3, 3, 12, 512], replicated, may hold values from -0.5 to 0.5
- out_bias: float32 [12], replicated, may hold values from -3 to 3
Outputs:
- latent: float32 [48, 256, 512], P('batch', 'rows'), parts along dimension 0
- bits_map: float32 [1024, 512], P(('batch', 'rows')), parts along dimension 0
- bits_mean: float32 [4], P('batch'), parts along dimension 0
The draws below stay inside these ranges and needn't reach their ends.
There are 4 independent parts, one for each index of `batch`. The reference program is written for one: setup_inputs(seed, part) draws one part's arguments, and reference() takes and returns one part's arrays. A program takes and returns all parts, laid end to end along the dimension named above; an argument that names none is the same for every part. Nothing has to cross between parts.
All inputs are finite; a program needn't handle non-finite values.
Results may differ from the reference program's by a relative error of at most 0.0044.
Values may be sent and summed in bfloat16 or wider, within the bound.
A program may use at most 64 MiB of HBM per device.

```python
import math
import jax
import jax.numpy as jnp
from jax import lax

C = 12
HID = 512
TERMS = 4
R = 2
W = 512
NR = 256
N_ROWS = 128


def draw_pixels(key, part):
    slab_key = jax.random.fold_in(key, 11)
    noise_key = jax.random.fold_in(key, 23)
    slab_count = NR // R
    log_scale = jax.random.uniform(slab_key, (slab_count,), jnp.float32, math.log(0.35), math.log(3.5))
    slab_scale = jnp.exp(log_scale)
    row_scale = jnp.repeat(slab_scale, R, total_repeat_length=NR)
    sample = jnp.clip(jax.random.normal(noise_key, (C, NR, W), jnp.float32), -4.0, 4.0)
    return jnp.clip(sample * row_scale[None, :, None], -8.0, 8.0)


def plant(array, stream_key, smallest, top_value):
    extent = array.shape
    spot = [jax.random.randint(jax.random.fold_in(stream_key, axis), (), 0, extent[axis]) for axis in range(len(extent))]
    array = array.at[tuple(spot)].set(smallest)
    longest = extent.index(max(extent))
    spot[longest] = (spot[longest] + 1) % extent[longest]
    return array.at[tuple(spot)].set(top_value)


def noise(stream_key, dims, spread, limit, held_as=jnp.bfloat16):
    entries = jax.random.normal(stream_key, dims, jnp.float32) * spread
    return jnp.minimum(jnp.maximum(entries, -limit), limit).astype(held_as)


def setup_inputs(seed: int = 0, part: int = 0) -> dict:
    streams_of = jax.random.split(jax.random.key(seed), 11)
    part_splits = jax.random.split(jax.random.fold_in(streams_of[10], part), 11)
    return {
        "pixels": draw_pixels(jax.random.fold_in(jax.random.fold_in(streams_of[10], part), 71), part),
        "probes": plant(jax.random.randint(part_splits[1], (C, NR, W), 0, 2), jax.random.fold_in(part_splits[1], 1), 0, 1).astype(jnp.int32),
        "in_weight": noise(streams_of[2], (3, 3, C, HID), (9 * C) ** -0.5, 0.625),
        "in_bias": noise(streams_of[3], (HID,), 0.5, 3.0, jnp.float32),
        "in_beta": jnp.clip(jnp.exp(jax.random.uniform(streams_of[4], (HID,), jnp.float32, math.log(0.5), math.log(4.0))), 0.5, 4.0),
        "mid_weight": noise(streams_of[5], (HID, HID), HID ** -0.5, 0.25),
        "mid_bias": noise(streams_of[6], (HID,), 0.5, 3.0, jnp.float32),
        "mid_beta": jnp.clip(jnp.exp(jax.random.uniform(streams_of[7], (HID,), jnp.float32, math.log(0.5), math.log(4.0))), 0.5, 4.0),
        "out_weight": noise(streams_of[8], (3, 3, C, HID), (HID // 4) ** -0.5, 0.5),
        "out_bias": noise(streams_of[9], (C,), 0.5, 3.0, jnp.float32),
    }


def activate(preact, gain_rate):
    gate_value = jax.nn.sigmoid(gain_rate * preact)
    return preact * gate_value / 1.1


def derivative(preact, gain_rate):
    gate_value = jax.nn.sigmoid(gain_rate * preact)
    return (gate_value + gain_rate * preact * gate_value * (1.0 - gate_value)) / 1.1


def correlate(preact, kernel, pattern, flipped):
    height = preact.shape[1] - 2
    breadth = preact.shape[2]
    padded = jnp.pad(preact, ((0, 0), (0, 0), (1, 1)))
    accumulated = jnp.zeros((), jnp.float32)
    for row_off in range(3):
        for col_off in range(3):
            if flipped:
                weights = kernel[2 - row_off, 2 - col_off]
            else:
                weights = kernel[row_off, col_off]
            shifted = padded[:, row_off:row_off + height, col_off:col_off + breadth].astype(jnp.float32)
            accumulated = accumulated + jnp.einsum(pattern, weights.astype(jnp.float32), shifted)
    return accumulated


def reference(pixels, probes, in_weight, in_bias, in_beta, mid_weight, mid_bias, mid_beta, out_weight, out_bias):
    stride = R * min(N_ROWS, 8)
    block_count = NR // stride
    starts = jnp.arange(block_count, dtype=jnp.int32) * stride
    in_rate = in_beta[:, None, None]
    mid_rate = mid_beta[:, None, None]
    padded_image = jnp.pad(pixels.astype(jnp.bfloat16), ((0, 0), (2, 2), (0, 0)))

    def hidden(row_start):
        window = lax.dynamic_slice_in_dim(padded_image, row_start, stride + 4, 1)
        first_pre = correlate(window, in_weight, 'ch,crw->hrw', False) + in_bias[:, None, None]
        first_act = activate(first_pre, in_rate).astype(jnp.bfloat16)
        second = jnp.einsum('hk,hrw->krw', mid_weight.astype(jnp.float32), first_act.astype(jnp.float32)) + mid_bias[:, None, None]
        row_ids = row_start - 1 + jnp.arange(stride + 2, dtype=jnp.int32)
        inside = jnp.where((row_ids >= 0) & (row_ids < NR), 1.0, 0.0).astype(jnp.float32)[None, :, None]
        return first_pre, second, inside

    def forward(row_start):
        first_pre, second, inside = hidden(row_start)
        second_act = (activate(second, mid_rate) * inside).astype(jnp.bfloat16)
        return correlate(second_act, out_weight, 'oh,hrw->orw', False) + out_bias[:, None, None]

    def stitch(blocks):
        return jnp.transpose(blocks, (1, 0, 2, 3)).reshape(C, NR, W)

    latent = pixels + stitch(lax.map(forward, starts))
    sign_field = (2 * probes - 1).astype(jnp.float32)
    vector = sign_field
    logdet = jnp.zeros((NR, W), jnp.float32)
    for term_index in range(1, TERMS + 1):
        padded_vector = jnp.pad(vector.astype(jnp.bfloat16), ((0, 0), (2, 2), (0, 0)))

        def pullback(row_start):
            first_pre, second, inside = hidden(row_start)
            window = lax.dynamic_slice_in_dim(padded_vector, row_start, stride + 4, 1)
            back_out = correlate(window, out_weight, 'oh,orw->hrw', True)
            back_mid = (back_out * derivative(second, mid_rate)).astype(jnp.bfloat16)
            back_in = jnp.einsum('hk,krw->hrw', mid_weight.astype(jnp.float32), back_mid.astype(jnp.float32))
            back_first = (back_in * derivative(first_pre, in_rate) * inside).astype(jnp.bfloat16)
            return correlate(back_first, in_weight, 'ch,hrw->crw', True)

        vector = stitch(lax.map(pullback, starts))
        logdet = logdet + ((-1.0) ** (term_index + 1) / term_index) * jnp.sum(vector * sign_field, axis=0)
    log_prior = -0.5 * jnp.sum(latent * latent, axis=0) - 0.5 * C * math.log(2.0 * math.pi)
    bits_map = 8.0 - (log_prior + logdet) / (C * math.log(2.0))
    bits_mean = (jnp.sum(bits_map) / (NR * W)).reshape(1)
    return latent, bits_map, bits_mean
```

```python
import functools
import math

import jax
import jax.numpy as jnp
from jax import lax
from jax.experimental import pallas as pl
from jax.experimental.pallas import tpu as pltpu
from jax.sharding import PartitionSpec as P

TERMS = 4
CH = 16
TAPS = 9 * CH
TILE = 256
MESH = pl.DeviceIdType.MESH


def from_left(x):
    lane = lax.broadcasted_iota(jnp.int32, x.shape, 1)
    return jnp.where(lane == 0, 0.0, pltpu.roll(x, 1, 1))


def from_right(x):
    last = x.shape[1] - 1
    lane = lax.broadcasted_iota(jnp.int32, x.shape, 1)
    return jnp.where(lane == last, 0.0, pltpu.roll(x, last, 1))


def fill_columns(columns, rows, flipped):
    width = rows[0].shape[1]
    for s, row in enumerate(rows):
        for j in range(3):
            if j == 1:
                piece = row
            elif (j == 0) != flipped:
                piece = from_left(row)
            else:
                piece = from_right(row)
            piece = piece.astype(jnp.bfloat16)
            for out_row in range(2):
                i = out_row + 2 - s if flipped else s - out_row
                if 0 <= i <= 2:
                    at = CH * (3 * i + j)
                    columns[at : at + CH, width * out_row : width * (out_row + 1)] = piece


def gather_taps(taps, width, flipped):
    def block(i, j, s):
        at = CH * (3 * i + j)
        return taps[at : at + CH, width * s : width * (s + 1)]

    result = []
    for d in range(4):
        total = None
        for j in range(3):
            part = None
            for s in range(2):
                i = d - s if flipped else s + 2 - d
                if 0 <= i <= 2:
                    value = block(i, j, s)
                    part = value if part is None else part + value
            if j != 1:
                part = from_right(part) if (j == 0) == flipped else from_left(part)
            total = part if total is None else total + part
        result.append(total)
    return result


def kernel(
    n_rows,
    group,
    pixels,
    probes,
    in_weight,
    in_bias,
    in_beta,
    mid_weight,
    mid_bias,
    mid_beta,
    out_weight,
    out_bias,
    latent_ref,
    bits_ref,
    mean_ref,
    pad_rows,
    weight_pad,
    in_plain,
    in_turned,
    out_plain,
    out_turned,
    mid_turned,
    columns,
    in_slope,
    mid_slope,
    act_a,
    act_b,
    act_c,
    taps,
    halo_send,
    halo_recv,
    lat_send,
    lat_recv,
    last_send,
    last_recv,
    mine,
    group_sums,
    ring_mine,
    ring_sums,
    send_sem,
    recv_sem,
    sum_send_sem,
    group_sem,
    ring_sem,
):
    channels, height, width = pixels.shape
    hidden = mid_weight.shape[0]
    me = lax.axis_index("rows")
    up = lax.rem(me + n_rows - 1, n_rows)
    down = lax.rem(me + 1, n_rows)
    ring = n_rows // group
    q = lax.rem(me, group)
    z = me // group
    group_peers = [z * group + lax.rem(q + d, group) for d in range(1, group)]
    ring_peers = [lax.rem(z + d, ring) * group + q for d in range(1, ring)]
    is_first = me == 0
    is_last = me == n_rows - 1

    barrier = pltpu.get_barrier_semaphore()
    peers = [up, down] + group_peers + ring_peers
    for peer in peers:
        pl.semaphore_signal(barrier, inc=1, device_id={"rows": peer}, device_id_type=MESH)

    pad_rows[...] = jnp.zeros_like(pad_rows)
    for r in range(height):
        pad_rows[r, 0:channels, :] = pixels[:, r, :]
        pad_rows[height + r, 0:channels, :] = (2 * probes[:, r, :] - 1).astype(jnp.float32)
    for side in range(2):
        halo_send[0, side, 0:CH, :] = pad_rows[side].astype(jnp.bfloat16)
        halo_send[0, side, CH : 2 * CH, :] = pad_rows[2 + side].astype(jnp.bfloat16)

    pl.semaphore_wait(barrier, len(peers))

    def exchange(send, recv, index):
        made = []
        for side, peer in enumerate((up, down)):
            copy = pltpu.make_async_remote_copy(
                src_ref=send.at[side],
                dst_ref=recv.at[1 - side],
                send_sem=send_sem.at[index, side],
                recv_sem=recv_sem.at[index, 1 - side],
                device_id={"rows": peer},
                device_id_type=MESH,
            )
            copy.start()
            made.append(copy)
        return made

    def finish(made):
        for copy in made:
            copy.wait()

    def inside(value, outside):
        return jnp.where(outside, 0.0, value)

    first = exchange(halo_send.at[0], halo_recv.at[0], 0)

    weight_pad[...] = jnp.zeros_like(weight_pad)
    for source, plain, turned in ((in_weight, in_plain, in_turned), (out_weight, out_plain, out_turned)):
        for i in range(3):
            for j in range(3):
                at = CH * (3 * i + j)
                weight_pad[at : at + channels, :] = source[i, j].astype(jnp.float32)
        whole = weight_pad[...]
        plain[...] = whole[:TAPS].astype(jnp.bfloat16)
        turned[...] = whole.T[:, :TAPS].astype(jnp.bfloat16)
    mid_turned[...] = mid_weight[...].T

    finish(first)
    top, bottom = (halo_recv[0, side].astype(jnp.float32) for side in range(2))
    pix_rows = [inside(top[:CH], is_first), pad_rows[0], pad_rows[1], inside(bottom[:CH], is_last)]
    signs = [inside(top[CH:], is_first), pad_rows[2], pad_rows[3], inside(bottom[CH:], is_last)]

    tiles = [slice(at, at + TILE) for at in range(0, height * width, TILE)]

    def dot(a, b):
        return jnp.dot(a, b, preferred_element_type=jnp.float32)

    scale = 0.5 / 1.1

    def lip(value, half_rate):
        half = half_rate * value
        t = jnp.tanh(half)
        gate = scale * (1.0 + t)
        return gate * value, gate * (1.0 + half * (1.0 - t))

    fill_columns(columns, pix_rows, False)
    in_b = in_bias[...]
    in_r = 0.5 * in_beta[...]
    mid_b = mid_bias[...]
    mid_r = 0.5 * mid_beta[...]
    for t in tiles:
        act, slope = lip(dot(in_turned[...], columns[:, t]) + in_b, in_r)
        act_a[:, t] = act.astype(jnp.bfloat16)
        in_slope[:, t] = slope
    for t in tiles:
        act, slope = lip(dot(mid_turned[...], act_a[:, t]) + mid_b, mid_r)
        act_c[:, t] = act.astype(jnp.bfloat16)
        mid_slope[:, t] = slope

    def pull_back(rows):
        fill_columns(columns, rows, True)
        for t in tiles:
            act_a[:, t] = (dot(out_turned[...], columns[:, t]) * mid_slope[:, t]).astype(jnp.bfloat16)
        for t in tiles:
            act_b[:, t] = (dot(mid_weight[...], act_a[:, t]) * in_slope[:, t]).astype(jnp.bfloat16)
        for t in tiles:
            taps[:, t] = dot(in_plain[...], act_b[:, t])
        return gather_taps(taps, width, True)

    vector = signs
    logdet = [jnp.zeros((1, width), jnp.float32) for _ in range(height)]
    log_prior = None
    latent_out = None
    for term in range(1, TERMS):
        parts = pull_back(vector)
        for side in range(2):
            for r in range(2):
                halo_send[term, side, CH * r : CH * (r + 1), :] = parts[2 * side + r].astype(jnp.bfloat16)
        moving = exchange(halo_send.at[term], halo_recv.at[term], term)
        if term == 1:
            for t in tiles:
                taps[:, t] = dot(out_plain[...], act_c[:, t])
            branch = gather_taps(taps, width, False)
            lat_send[0] = branch[0].astype(jnp.bfloat16)
            lat_send[1] = branch[3].astype(jnp.bfloat16)
            lat_moving = exchange(lat_send, lat_recv, TERMS)
        if term == 2:
            finish(lat_moving)
            outer = [inside(lat_recv[side].astype(jnp.float32), where) for side, where in enumerate((is_first, is_last))]
            log_prior = []
            for r in range(height):
                whole = branch[1 + r] + outer[r]
                latent = pixels[:, r, :] + (whole[:channels] + out_bias[...])
                latent_ref[:, r, :] = latent
                log_prior.append(-0.5 * jnp.sum(latent * latent, axis=0, keepdims=True))
        finish(moving)
        top = inside(halo_recv[term, 0].astype(jnp.float32), is_first)
        bottom = inside(halo_recv[term, 1].astype(jnp.float32), is_last)
        vector = [
            inside(parts[0], is_first) + top[:CH],
            parts[1] + top[CH:],
            parts[2] + bottom[:CH],
            inside(parts[3], is_last) + bottom[CH:],
        ]
        weight = (-1.0) ** (term + 1) / term
        for r in range(height):
            logdet[r] = logdet[r] + weight * jnp.sum(vector[1 + r] * signs[1 + r], axis=0, keepdims=True)

    parts = pull_back(vector)
    weight = (-1.0) ** (TERMS + 1) / TERMS
    dots = [weight * jnp.sum(part * sign, axis=0, keepdims=True) for part, sign in zip(parts, signs)]
    last_send[0] = dots[0]
    last_send[1] = dots[3]
    moving = exchange(last_send, last_recv, TERMS + 1)
    known = [log_prior[r] + logdet[r] + dots[1 + r] for r in range(height)]
    total = (known[0] + known[1]) + (dots[0] + dots[3])
    lanes = total[:, 0:128]
    for at in range(128, width, 128):
        lanes = lanes + total[:, at : at + 128]

    def spread(value, own, slots, slot, others, sems, send_at):
        own[...] = value
        made = []
        for d, peer in enumerate(others):
            copy = pltpu.make_async_remote_copy(
                src_ref=own,
                dst_ref=slots.at[slot],
                send_sem=sum_send_sem.at[send_at + d],
                recv_sem=sems.at[slot],
                device_id={"rows": peer},
                device_id_type=MESH,
            )
            copy.start()
            made.append(copy)
        slots[slot] = value
        return made

    def collect(own, slots, slot, sems, count):
        for d in range(1, count):
            other = lax.rem(slot + d, count)
            pltpu.make_async_copy(own, slots.at[other], sems.at[other]).wait()
        value = slots[0]
        for d in range(1, count):
            value = value + slots[d]
        return value

    sums = spread(lanes, mine, group_sums, q, group_peers, group_sem, 0)
    lanes = collect(mine, group_sums, q, group_sem, group)
    sums += spread(lanes, ring_mine, ring_sums, z, ring_peers, ring_sem, group - 1)

    finish(moving)
    spare = [inside(last_recv[side], where) for side, where in enumerate((is_first, is_last))]
    base = 8.0 + 0.5 * math.log(2.0 * math.pi) / math.log(2.0)
    rate = 1.0 / (channels * math.log(2.0))
    for r in range(height):
        bits_ref[r : r + 1, :] = base - rate * (known[r] + spare[r])

    lanes = collect(ring_mine, ring_sums, z, ring_sem, ring)
    mean_ref[0] = base - jnp.sum(lanes) * (rate / (n_rows * height * width))
    for copy in sums:
        copy.wait_send()


def solution(mesh):
    n_rows = mesh.shape["rows"]
    group = min(8, n_rows // 2)
    ring = n_rows // group

    def per_device(
        pixels, probes, in_weight, in_bias, in_beta, mid_weight, mid_bias, mid_beta, out_weight, out_bias
    ):
        channels, height, width = pixels.shape
        hidden = mid_weight.shape[0]
        area = height * width
        f32, bf16 = jnp.float32, jnp.bfloat16
        vmem = pl.BlockSpec(memory_space=pltpu.VMEM)
        return pl.pallas_call(
            functools.partial(kernel, n_rows, group),
            out_shape=(
                jax.ShapeDtypeStruct((channels, height, width), f32),
                jax.ShapeDtypeStruct((height, width), f32),
                jax.ShapeDtypeStruct((1,), f32),
            ),
            in_specs=[vmem] * 10,
            out_specs=(vmem, vmem, pl.BlockSpec(memory_space=pltpu.SMEM)),
            scratch_shapes=[
                pltpu.VMEM((4, CH, width), f32),
                pltpu.VMEM((256, hidden), f32),
                pltpu.VMEM((TAPS, hidden), bf16),
                pltpu.VMEM((hidden, TAPS), bf16),
                pltpu.VMEM((TAPS, hidden), bf16),
                pltpu.VMEM((hidden, TAPS), bf16),
                pltpu.VMEM((hidden, hidden), bf16),
                pltpu.VMEM((TAPS, area), bf16),
                pltpu.VMEM((hidden, area), f32),
                pltpu.VMEM((hidden, area), f32),
                pltpu.VMEM((hidden, area), bf16),
                pltpu.VMEM((hidden, area), bf16),
                pltpu.VMEM((hidden, area), bf16),
                pltpu.VMEM((TAPS, area), f32),
                pltpu.VMEM((TERMS, 2, 2 * CH, width), bf16),
                pltpu.VMEM((TERMS, 2, 2 * CH, width), bf16),
                pltpu.VMEM((2, CH, width), bf16),
                pltpu.VMEM((2, CH, width), bf16),
                pltpu.VMEM((2, 1, width), f32),
                pltpu.VMEM((2, 1, width), f32),
                pltpu.VMEM((1, 128), f32),
                pltpu.VMEM((group, 1, 128), f32),
                pltpu.VMEM((1, 128), f32),
                pltpu.VMEM((ring, 1, 128), f32),
                pltpu.SemaphoreType.DMA((TERMS + 2, 2)),
                pltpu.SemaphoreType.DMA((TERMS + 2, 2)),
                pltpu.SemaphoreType.DMA((group + ring - 2,)),
                pltpu.SemaphoreType.DMA((group,)),
                pltpu.SemaphoreType.DMA((ring,)),
            ],
            compiler_params=pltpu.CompilerParams(
                collective_id=0, has_side_effects=True, vmem_limit_bytes=40 * 1024 * 1024
            ),
        )(
            pixels,
            probes,
            in_weight,
            in_bias[:, None],
            in_beta[:, None],
            mid_weight,
            mid_bias[:, None],
            mid_beta[:, None],
            out_weight,
            out_bias[:, None],
        )

    placed = (P("batch", "rows", None),) * 2 + (P(),) * 8
    return jax.shard_map(
        per_device,
        mesh=mesh,
        in_specs=placed,
        out_specs=(P("batch", "rows", None), P(("batch", "rows"), None), P("batch")),
        check_vma=False,
    )
```

```python
import functools
import math

import jax
import jax.numpy as jnp
from jax import lax
from jax.experimental import pallas as pl
from jax.experimental.pallas import tpu as pltpu
from jax.sharding import PartitionSpec as P

TERMS = 4
CH = 16
TAPS = 9 * CH
TILE = 256
MESH = pl.DeviceIdType.MESH


def from_left(x):
    lane = lax.broadcasted_iota(jnp.int32, x.shape, 1)
    return jnp.where(lane == 0, 0.0, pltpu.roll(x, 1, 1))


def from_right(x):
    last = x.shape[1] - 1
    lane = lax.broadcasted_iota(jnp.int32, x.shape, 1)
    return jnp.where(lane == last, 0.0, pltpu.roll(x, last, 1))


def fill_columns(columns, rows, flipped):
    width = rows[0].shape[1]
    for s, row in enumerate(rows):
        for j in range(3):
            if j == 1:
                piece = row
            elif (j == 0) != flipped:
                piece = from_left(row)
            else:
                piece = from_right(row)
            piece = piece.astype(jnp.bfloat16)
            for out_row in range(2):
                i = out_row + 2 - s if flipped else s - out_row
                if 0 <= i <= 2:
                    at = CH * (3 * i + j)
                    columns[at : at + CH, width * out_row : width * (out_row + 1)] = piece


def gather_taps(taps, width, flipped):
    def block(i, j, s):
        at = CH * (3 * i + j)
        return taps[at : at + CH, width * s : width * (s + 1)]

    result = []
    for d in range(4):
        total = None
        for j in range(3):
            part = None
            for s in range(2):
                i = d - s if flipped else s + 2 - d
                if 0 <= i <= 2:
                    value = block(i, j, s)
                    part = value if part is None else part + value
            if j != 1:
                part = from_right(part) if (j == 0) == flipped else from_left(part)
            total = part if total is None else total + part
        result.append(total)
    return result


def kernel(
    n_rows,
    group,
    pixels_hbm,
    probes_hbm,
    in_weight_hbm,
    in_bias_hbm,
    in_beta_hbm,
    mid_weight_hbm,
    mid_bias_hbm,
    mid_beta_hbm,
    out_weight_hbm,
    out_bias_hbm,
    latent_ref,
    bits_ref,
    mean_ref,
    pixels,
    probes,
    in_weight,
    in_bias,
    in_beta,
    mid_weight,
    mid_bias,
    mid_beta,
    out_weight,
    out_bias,
    load_sem,
    pad_rows,
    small_pad,
    weight_pad,
    in_plain,
    in_turned,
    out_plain,
    out_turned,
    mid_turned,
    columns,
    in_slope,
    mid_slope,
    act_a,
    act_b,
    act_c,
    taps,
    halo_send,
    halo_recv,
    pair_send,
    pair_recv,
    lat_send,
    lat_recv,
    last_send,
    last_recv,
    mine,
    group_sums,
    ring_mine,
    ring_sums,
    send_sem,
    recv_sem,
    sum_send_sem,
    group_sem,
    ring_sem,
    known_sem,
):
    channels, height, width = pixels.shape
    me = lax.axis_index("rows")
    up = lax.rem(me + n_rows - 1, n_rows)
    down = lax.rem(me + 1, n_rows)
    ring = n_rows // group
    q = lax.rem(me, group)
    z = me // group
    group_peers = [z * group + lax.rem(q + d, group) for d in range(1, group)]
    ring_peers = [lax.rem(z + d, ring) * group + q for d in range(1, ring)]
    is_first = me == 0
    is_last = me == n_rows - 1

    sources = (
        pixels_hbm,
        probes_hbm,
        in_bias_hbm,
        in_beta_hbm,
        mid_bias_hbm,
        mid_beta_hbm,
        out_bias_hbm,
        in_weight_hbm,
        out_weight_hbm,
        mid_weight_hbm,
    )
    places = (pixels, probes, in_bias, in_beta, mid_bias, mid_beta, out_bias, in_weight, out_weight, mid_weight)
    loads = [
        pltpu.make_async_copy(source, place, load_sem.at[k]) for k, (source, place) in enumerate(zip(sources, places))
    ]
    for load in loads[:2]:
        load.start()

    def signal(sem, peer):
        pl.semaphore_signal(sem, inc=1, device_id={"rows": peer}, device_id_type=MESH)

    def around(step):
        return [lax.rem(z + d, ring) * group + q for d in (step, ring - step)]

    barrier = pltpu.get_barrier_semaphore()
    greeted = [up, down] + group_peers + around(1)
    for peer in greeted:
        signal(barrier, peer)
    for load in loads[2:]:
        load.start()

    steps = []
    while 2 ** len(steps) < ring // 2:
        steps.append(2 ** len(steps))

    def spread_word(k):
        if k < len(steps):
            for peer in around(steps[k]):
                signal(known_sem.at[k], peer)

    def hear_word(k):
        if k < len(steps):
            pl.semaphore_wait(known_sem.at[k], 2)

    loads[0].wait()
    loads[1].wait()
    pad_rows[...] = jnp.zeros_like(pad_rows)
    for r in range(height):
        pad_rows[r, 0:channels, :] = pixels[:, r, :]
        pad_rows[height + r, 0:channels, :] = (2 * probes[:, r, :] - 1).astype(jnp.float32)
    for side in range(2):
        halo_send[0, side, 0:CH, :] = pad_rows[side].astype(jnp.bfloat16)
        halo_send[0, side, CH : 2 * CH, :] = pad_rows[2 + side].astype(jnp.bfloat16)

    pl.semaphore_wait(barrier, len(greeted))

    def exchange(send, recv, index):
        made = []
        for side, peer in enumerate((up, down)):
            copy = pltpu.make_async_remote_copy(
                src_ref=send.at[side],
                dst_ref=recv.at[1 - side],
                send_sem=send_sem.at[index, side],
                recv_sem=recv_sem.at[index, 1 - side],
                device_id={"rows": peer},
                device_id_type=MESH,
            )
            copy.start()
            made.append(copy)
        return made

    def finish(made):
        for copy in made:
            copy.wait()

    def inside(value, outside):
        return jnp.where(outside, 0.0, value)

    first = exchange(halo_send.at[0], halo_recv.at[0], 0)
    spread_word(0)

    for load in loads[2:]:
        load.wait()
    small_pad[...] = jnp.zeros_like(small_pad)
    for k, vector_ref in enumerate((in_bias, in_beta, mid_bias, mid_beta)):
        small_pad[k : k + 1, :] = vector_ref[...]
    small_pad[4:5, 0:channels] = out_bias[...]
    small = small_pad[...].T
    in_b, in_r, mid_b, mid_r = (small[:, k : k + 1] for k in range(4))
    in_r = 0.5 * in_r
    mid_r = 0.5 * mid_r
    out_b = small[:channels, 4:5]

    weight_pad[...] = jnp.zeros_like(weight_pad)
    for source, plain, turned in ((in_weight, in_plain, in_turned), (out_weight, out_plain, out_turned)):
        for i in range(3):
            for j in range(3):
                at = CH * (3 * i + j)
                weight_pad[at : at + channels, :] = source[i, j].astype(jnp.float32)
        whole = weight_pad[...]
        plain[...] = whole[:TAPS].astype(jnp.bfloat16)
        turned[...] = whole.T[:, :TAPS].astype(jnp.bfloat16)
    mid_turned[...] = mid_weight[...].T

    finish(first)
    top, bottom = (halo_recv[0, side].astype(jnp.float32) for side in range(2))
    pix_rows = [inside(top[:CH], is_first), pad_rows[0], pad_rows[1], inside(bottom[:CH], is_last)]
    signs = [inside(top[CH:], is_first), pad_rows[2], pad_rows[3], inside(bottom[CH:], is_last)]

    tiles = [slice(at, at + TILE) for at in range(0, height * width, TILE)]

    def dot(a, b):
        return jnp.dot(a, b, preferred_element_type=jnp.float32)

    scale = 0.5 / 1.1

    def lip(value, half_rate):
        half = half_rate * value
        t = jnp.tanh(half)
        gate = scale * (1.0 + t)
        return gate * value, gate * (1.0 + half * (1.0 - t))

    fill_columns(columns, pix_rows, False)
    for t in tiles:
        act, slope = lip(dot(in_turned[...], columns[:, t]) + in_b, in_r)
        act_a[:, t] = act.astype(jnp.bfloat16)
        in_slope[:, t] = slope
    for t in tiles:
        act, slope = lip(dot(mid_turned[...], act_a[:, t]) + mid_b, mid_r)
        act_c[:, t] = act.astype(jnp.bfloat16)
        mid_slope[:, t] = slope

    def pull_back(rows):
        fill_columns(columns, rows, True)
        for t in tiles:
            act_a[:, t] = (dot(out_turned[...], columns[:, t]) * mid_slope[:, t]).astype(jnp.bfloat16)
        for t in tiles:
            act_b[:, t] = (dot(mid_weight[...], act_a[:, t]) * in_slope[:, t]).astype(jnp.bfloat16)
        for t in tiles:
            taps[:, t] = dot(in_plain[...], act_b[:, t])
        return gather_taps(taps, width, True)

    def push(rows):
        fill_columns(columns, rows, False)
        for t in tiles:
            act_a[:, t] = (dot(in_turned[...], columns[:, t]) * in_slope[:, t]).astype(jnp.bfloat16)
        for t in tiles:
            act_b[:, t] = (dot(mid_turned[...], act_a[:, t]) * mid_slope[:, t]).astype(jnp.bfloat16)
        for t in tiles:
            taps[:, t] = dot(out_plain[...], act_b[:, t])
        return gather_taps(taps, width, False)

    def send_parts(parts, send, recv, index):
        for side in range(2):
            for r in range(2):
                send[side, CH * r : CH * (r + 1), :] = parts[2 * side + r].astype(jnp.bfloat16)
        return exchange(send, recv, index)

    def whole_rows(parts, recv, moving):
        finish(moving)
        top = inside(recv[0].astype(jnp.float32), is_first)
        bottom = inside(recv[1].astype(jnp.float32), is_last)
        return [
            inside(parts[0], is_first) + top[:CH],
            parts[1] + top[CH:],
            parts[2] + bottom[:CH],
            inside(parts[3], is_last) + bottom[CH:],
        ]

    def coefficient(term):
        return (-1.0) ** (term + 1) / term

    def add_term(logdet, rows, term):
        return [
            logdet[r] + coefficient(term) * jnp.sum(rows[1 + r] * signs[1 + r], axis=0, keepdims=True)
            for r in range(height)
        ]

    logdet = [jnp.zeros((1, width), jnp.float32) for _ in range(height)]

    parts = pull_back(signs)
    moving = send_parts(parts, halo_send.at[1], halo_recv.at[1], 1)
    hear_word(0)
    spread_word(1)
    for t in tiles:
        taps[:, t] = dot(out_plain[...], act_c[:, t])
    branch = gather_taps(taps, width, False)
    lat_send[0] = branch[0].astype(jnp.bfloat16)
    lat_send[1] = branch[3].astype(jnp.bfloat16)
    lat_moving = exchange(lat_send, lat_recv, TERMS)
    pushed_1 = push(signs)
    pair_moving = send_parts(pushed_1, pair_send, pair_recv, TERMS + 2)
    hear_word(1)
    spread_word(2)
    vector = whole_rows(parts, halo_recv.at[1], moving)

    parts = pull_back(vector)
    moving = send_parts(parts, halo_send.at[2], halo_recv.at[2], 2)
    logdet = add_term(logdet, vector, 1)
    finish(lat_moving)
    outer = [inside(lat_recv[side].astype(jnp.float32), where) for side, where in enumerate((is_first, is_last))]
    log_prior = []
    for r in range(height):
        whole = branch[1 + r] + outer[r]
        latent = pixels[:, r, :] + (whole[:channels] + out_b)
        latent_ref[:, r, :] = latent
        log_prior.append(-0.5 * jnp.sum(latent * latent, axis=0, keepdims=True))
    pushed_2 = push(whole_rows(pushed_1, pair_recv, pair_moving))
    hear_word(2)
    vector = whole_rows(parts, halo_recv.at[2], moving)

    logdet = add_term(logdet, vector, 2)
    total = (log_prior[0] + logdet[0]) + (log_prior[1] + logdet[1])
    later = None
    for d in range(4):
        both = (coefficient(3) * pushed_1[d] + coefficient(4) * pushed_2[d]) * vector[d]
        later = both if later is None else later + both
    total = total + jnp.sum(later, axis=0, keepdims=True)
    lanes = total[:, 0:128]
    for at in range(128, width, 128):
        lanes = lanes + total[:, at : at + 128]

    def spread(value, own, slots, slot, others, sems, send_at):
        own[...] = value
        made = []
        for d, peer in enumerate(others):
            copy = pltpu.make_async_remote_copy(
                src_ref=own,
                dst_ref=slots.at[slot],
                send_sem=sum_send_sem.at[send_at + d],
                recv_sem=sems.at[slot],
                device_id={"rows": peer},
                device_id_type=MESH,
            )
            copy.start()
            made.append(copy)
        slots[slot] = value
        return made

    def collect(own, slots, slot, sems, count):
        for d in range(1, count):
            other = lax.rem(slot + d, count)
            pltpu.make_async_copy(own, slots.at[other], sems.at[other]).wait()
        value = slots[0]
        for d in range(1, count):
            value = value + slots[d]
        return value

    sums = spread(lanes, mine, group_sums, q, group_peers, group_sem, 0)

    parts = pull_back(vector)
    moving = send_parts(parts, halo_send.at[3], halo_recv.at[3], 3)
    lanes = collect(mine, group_sums, q, group_sem, group)
    sums += spread(lanes, ring_mine, ring_sums, z, ring_peers, ring_sem, group - 1)
    vector = whole_rows(parts, halo_recv.at[3], moving)

    parts = pull_back(vector)
    dots = [coefficient(4) * jnp.sum(part * sign, axis=0, keepdims=True) for part, sign in zip(parts, signs)]
    last_send[0] = dots[0]
    last_send[1] = dots[3]
    moving = exchange(last_send, last_recv, TERMS + 1)
    logdet = add_term(logdet, vector, 3)
    known = [log_prior[r] + logdet[r] + dots[1 + r] for r in range(height)]
    finish(moving)
    spare = [inside(last_recv[side], where) for side, where in enumerate((is_first, is_last))]
    base = 8.0 + 0.5 * math.log(2.0 * math.pi) / math.log(2.0)
    rate = 1.0 / (channels * math.log(2.0))
    for r in range(height):
        bits_ref[r : r + 1, :] = base - rate * (known[r] + spare[r])

    lanes = collect(ring_mine, ring_sums, z, ring_sem, ring)
    mean_ref[0] = base - jnp.sum(lanes) * (rate / (n_rows * height * width))
    for copy in sums:
        copy.wait_send()


def solution(mesh):
    n_rows = mesh.shape["rows"]
    group = min(8, n_rows // 2)
    ring = n_rows // group

    def per_device(
        pixels, probes, in_weight, in_bias, in_beta, mid_weight, mid_bias, mid_beta, out_weight, out_bias
    ):
        channels, height, width = pixels.shape
        hidden = mid_weight.shape[0]
        area = height * width
        f32, bf16 = jnp.float32, jnp.bfloat16
        vmem = pl.BlockSpec(memory_space=pltpu.VMEM)
        return pl.pallas_call(
            functools.partial(kernel, n_rows, group),
            out_shape=(
                jax.ShapeDtypeStruct((channels, height, width), f32),
                jax.ShapeDtypeStruct((height, width), f32),
                jax.ShapeDtypeStruct((1,), f32),
            ),
            in_specs=[pl.BlockSpec(memory_space=pltpu.HBM)] * 10,
            out_specs=(vmem, vmem, pl.BlockSpec(memory_space=pltpu.SMEM)),
            scratch_shapes=[
                pltpu.VMEM((channels, height, width), f32),
                pltpu.VMEM((channels, height, width), probes.dtype),
                pltpu.VMEM(in_weight.shape, bf16),
                pltpu.VMEM((1, hidden), f32),
                pltpu.VMEM((1, hidden), f32),
                pltpu.VMEM((hidden, hidden), bf16),
                pltpu.VMEM((1, hidden), f32),
                pltpu.VMEM((1, hidden), f32),
                pltpu.VMEM(out_weight.shape, bf16),
                pltpu.VMEM((1, channels), f32),
                pltpu.SemaphoreType.DMA((10,)),
                pltpu.VMEM((4, CH, width), f32),
                pltpu.VMEM((128, hidden), f32),
                pltpu.VMEM((256, hidden), f32),
                pltpu.VMEM((TAPS, hidden), bf16),
                pltpu.VMEM((hidden, TAPS), bf16),
                pltpu.VMEM((TAPS, hidden), bf16),
                pltpu.VMEM((hidden, TAPS), bf16),
                pltpu.VMEM((hidden, hidden), bf16),
                pltpu.VMEM((TAPS, area), bf16),
                pltpu.VMEM((hidden, area), f32),
                pltpu.VMEM((hidden, area), f32),
                pltpu.VMEM((hidden, area), bf16),
                pltpu.VMEM((hidden, area), bf16),
                pltpu.VMEM((hidden, area), bf16),
                pltpu.VMEM((TAPS, area), f32),
                pltpu.VMEM((TERMS, 2, 2 * CH, width), bf16),
                pltpu.VMEM((TERMS, 2, 2 * CH, width), bf16),
                pltpu.VMEM((2, 2 * CH, width), bf16),
                pltpu.VMEM((2, 2 * CH, width), bf16),
                pltpu.VMEM((2, CH, width), bf16),
                pltpu.VMEM((2, CH, width), bf16),
                pltpu.VMEM((2, 1, width), f32),
                pltpu.VMEM((2, 1, width), f32),
                pltpu.VMEM((1, 128), f32),
                pltpu.VMEM((group, 1, 128), f32),
                pltpu.VMEM((1, 128), f32),
                pltpu.VMEM((ring, 1, 128), f32),
                pltpu.SemaphoreType.DMA((TERMS + 3, 2)),
                pltpu.SemaphoreType.DMA((TERMS + 3, 2)),
                pltpu.SemaphoreType.DMA((group + ring - 2,)),
                pltpu.SemaphoreType.DMA((group,)),
                pltpu.SemaphoreType.DMA((ring,)),
                pltpu.SemaphoreType.REGULAR((3,)),
            ],
            compiler_params=pltpu.CompilerParams(
                collective_id=0, has_side_effects=True, vmem_limit_bytes=60 * 1024 * 1024
            ),
        )(
            pixels,
            probes,
            in_weight,
            in_bias[None, :],
            in_beta[None, :],
            mid_weight,
            mid_bias[None, :],
            mid_beta[None, :],
            out_weight,
            out_bias[None, :],
        )

    placed = (P("batch", "rows", None),) * 2 + (P(),) * 8
    return jax.shard_map(
        per_device,
        mesh=mesh,
        in_specs=placed,
        out_specs=(P("batch", "rows", None), P(("batch", "rows"), None), P("batch")),
        check_vma=False,
    )
```

```python
import functools
import math

import jax
import jax.numpy as jnp
from jax import lax
from jax.experimental import pallas as pl
from jax.experimental.pallas import tpu as pltpu
from jax.sharding import PartitionSpec as P

TERMS = 4
CH = 16
TAPS = 9 * CH
TILE = 256
MESH = pl.DeviceIdType.MESH


def from_left(x):
    lane = lax.broadcasted_iota(jnp.int32, x.shape, 1)
    return jnp.where(lane == 0, 0.0, pltpu.roll(x, 1, 1))


def from_right(x):
    last = x.shape[1] - 1
    lane = lax.broadcasted_iota(jnp.int32, x.shape, 1)
    return jnp.where(lane == last, 0.0, pltpu.roll(x, last, 1))


def fill_columns(columns, rows, flipped):
    width = rows[0].shape[1]
    for s, row in enumerate(rows):
        for j in range(3):
            if j == 1:
                piece = row
            elif (j == 0) != flipped:
                piece = from_left(row)
            else:
                piece = from_right(row)
            piece = piece.astype(jnp.bfloat16)
            for out_row in range(2):
                i = out_row + 2 - s if flipped else s - out_row
                if 0 <= i <= 2:
                    at = CH * (3 * i + j)
                    columns[at : at + CH, width * out_row : width * (out_row + 1)] = piece


def gather_taps(taps, width, flipped):
    def block(i, j, s):
        at = CH * (3 * i + j)
        return taps[at : at + CH, width * s : width * (s + 1)]

    result = []
    for d in range(4):
        total = None
        for j in range(3):
            part = None
            for s in range(2):
                i = d - s if flipped else s + 2 - d
                if 0 <= i <= 2:
                    value = block(i, j, s)
                    part = value if part is None else part + value
            if j != 1:
                part = from_right(part) if (j == 0) == flipped else from_left(part)
            total = part if total is None else total + part
        result.append(total)
    return result


def kernel(
    n_rows,
    group,
    pixels_hbm,
    probes_hbm,
    in_weight_hbm,
    in_bias_hbm,
    in_beta_hbm,
    mid_weight_hbm,
    mid_bias_hbm,
    mid_beta_hbm,
    out_weight_hbm,
    out_bias_hbm,
    latent_ref,
    bits_ref,
    mean_ref,
    pixels,
    probes,
    in_weight,
    in_bias,
    in_beta,
    mid_weight,
    mid_bias,
    mid_beta,
    out_weight,
    out_bias,
    load_sem,
    pad_rows,
    small_pad,
    weight_pad,
    in_plain,
    in_turned,
    out_plain,
    out_turned,
    mid_turned,
    columns,
    in_slope,
    mid_slope,
    act_a,
    act_b,
    act_c,
    taps,
    slab_send,
    slab_own,
    slab_above,
    slab_below,
    halo_send,
    halo_recv,
    pair_send,
    pair_recv,
    lat_send,
    lat_recv,
    lat_own_send,
    lat_own,
    last_send,
    last_recv,
    last_own_send,
    last_own,
    mine,
    group_sums,
    ring_mine,
    ring_sums,
    send_sem,
    recv_sem,
    three_send,
    three_recv,
    sum_send_sem,
    group_sem,
    ring_sem,
    known_sem,
):
    channels, height, width = pixels.shape
    me = lax.axis_index("rows")
    ring = n_rows // group
    q = lax.rem(me, group)
    z = me // group
    group_peers = [z * group + lax.rem(q + d, group) for d in range(1, group)]
    ring_peers = [lax.rem(z + d, ring) * group + q for d in range(1, ring)]

    def worker(slab):
        layer = slab // group
        s = lax.rem(slab, group)
        back = group - 1 - s
        swapped = back + 1 - 2 * lax.rem(back, 2)
        return layer * group + s + lax.rem(layer, 2) * (swapped - s)

    def step(slab, by):
        return lax.rem(slab + n_rows + by, n_rows)

    slab = worker(me)
    stays = slab == me
    owners = (step(slab, -1), slab, step(slab, 1))
    workers = (worker(step(me, -1)), slab, worker(step(me, 1)))
    up, down = worker(owners[0]), worker(owners[2])
    edges_slab = (slab == 0, slab == n_rows - 1)
    edges_own = (me == 0, me == n_rows - 1)

    sources = (
        pixels_hbm,
        probes_hbm,
        in_bias_hbm,
        in_beta_hbm,
        mid_bias_hbm,
        mid_beta_hbm,
        out_bias_hbm,
        in_weight_hbm,
        out_weight_hbm,
        mid_weight_hbm,
    )
    places = (pixels, probes, in_bias, in_beta, mid_bias, mid_beta, out_bias, in_weight, out_weight, mid_weight)
    loads = [
        pltpu.make_async_copy(source, place, load_sem.at[k]) for k, (source, place) in enumerate(zip(sources, places))
    ]
    for load in loads[:2]:
        load.start()

    def signal(sem, peer):
        pl.semaphore_signal(sem, inc=1, device_id={"rows": peer}, device_id_type=MESH)

    def around(by):
        return [lax.rem(z + d, ring) * group + q for d in (by, ring - by)]

    barrier = pltpu.get_barrier_semaphore()
    greeted = [up, down, owners[0], owners[2], workers[0], workers[2]] + group_peers + around(1)
    for peer in greeted:
        signal(barrier, peer)
    for load in loads[2:]:
        load.start()

    steps = []
    while 2 ** len(steps) < ring // 2:
        steps.append(2 ** len(steps))

    def spread_word(k):
        if k < len(steps):
            for peer in around(steps[k]):
                signal(known_sem.at[k], peer)

    def hear_word(k):
        if k < len(steps):
            pl.semaphore_wait(known_sem.at[k], 2)

    loads[0].wait()
    loads[1].wait()
    pad_rows[...] = jnp.zeros_like(pad_rows)
    for r in range(height):
        pad_rows[2 * r, 0:channels, :] = pixels[:, r, :]
        pad_rows[2 * r + 1, 0:channels, :] = (2 * probes[:, r, :] - 1).astype(jnp.float32)
    for k in range(2 * height):
        slab_send[CH * k : CH * (k + 1), :] = pad_rows[k].astype(jnp.bfloat16)

    pl.semaphore_wait(barrier, len(greeted))

    def remote(source, place, sent, arrived, peer):
        return pltpu.make_async_remote_copy(
            src_ref=source,
            dst_ref=place,
            send_sem=sent,
            recv_sem=arrived,
            device_id={"rows": peer},
            device_id_type=MESH,
        )

    def exchange(send, recv, index):
        made = [
            remote(send.at[side], recv.at[1 - side], send_sem.at[index, side], recv_sem.at[index, 1 - side], peer)
            for side, peer in enumerate((up, down))
        ]
        for copy in made:
            copy.start()
        return made

    def finish(made):
        for copy in made:
            copy.wait()

    def hand_over(sources, places, peers, index):
        made = [
            remote(source, place, three_send.at[index, k], three_recv.at[index, k], peer)
            for k, (source, place, peer) in enumerate(zip(sources, places, peers))
        ]
        made[0].start()
        made[2].start()
        local = pltpu.make_async_copy(sources[1], places[1], three_recv.at[index, 1])

        @pl.when(jnp.logical_not(stays))
        def _():
            made[1].start()

        @pl.when(stays)
        def _():
            local.start()

        return made

    def take_over(made):
        for copy in made:
            copy.wait_recv()
        made[0].wait_send()
        made[2].wait_send()

        @pl.when(jnp.logical_not(stays))
        def _():
            made[1].wait_send()

    def inside(value, outside):
        return jnp.where(outside, 0.0, value)

    first = hand_over(
        (slab_send.at[0 : 2 * CH], slab_send, slab_send.at[2 * CH : 4 * CH]),
        (slab_below, slab_own, slab_above),
        workers,
        0,
    )
    spread_word(0)

    for load in loads[2:]:
        load.wait()
    small_pad[...] = jnp.zeros_like(small_pad)
    for k, vector_ref in enumerate((in_bias, in_beta, mid_bias, mid_beta)):
        small_pad[k : k + 1, :] = vector_ref[...]
    small_pad[4:5, 0:channels] = out_bias[...]
    small = small_pad[...].T
    in_b, in_r, mid_b, mid_r = (small[:, k : k + 1] for k in range(4))
    in_r = 0.5 * in_r
    mid_r = 0.5 * mid_r
    out_b = small[:channels, 4:5]

    weight_pad[...] = jnp.zeros_like(weight_pad)
    for source, plain, turned in ((in_weight, in_plain, in_turned), (out_weight, out_plain, out_turned)):
        for i in range(3):
            for j in range(3):
                at = CH * (3 * i + j)
                weight_pad[at : at + channels, :] = source[i, j].astype(jnp.float32)
        whole = weight_pad[...]
        plain[...] = whole[:TAPS].astype(jnp.bfloat16)
        turned[...] = whole.T[:, :TAPS].astype(jnp.bfloat16)
    mid_turned[...] = mid_weight[...].T

    take_over(first)
    above, own, below = (ref[...].astype(jnp.float32) for ref in (slab_above, slab_own, slab_below))
    pix_rows = [inside(above[:CH], edges_slab[0]), own[:CH], own[2 * CH : 3 * CH], inside(below[:CH], edges_slab[1])]
    signs = [inside(above[CH:], edges_slab[0]), own[CH : 2 * CH], own[3 * CH :], inside(below[CH:], edges_slab[1])]

    tiles = [slice(at, at + TILE) for at in range(0, height * width, TILE)]

    def dot(a, b):
        return jnp.dot(a, b, preferred_element_type=jnp.float32)

    scale = 0.5 / 1.1

    def lip(value, half_rate):
        half = half_rate * value
        t = jnp.tanh(half)
        gate = scale * (1.0 + t)
        return gate * value, gate * (1.0 + half * (1.0 - t))

    fill_columns(columns, pix_rows, False)
    for t in tiles:
        act, slope = lip(dot(in_turned[...], columns[:, t]) + in_b, in_r)
        act_a[:, t] = act.astype(jnp.bfloat16)
        in_slope[:, t] = slope
    for t in tiles:
        act, slope = lip(dot(mid_turned[...], act_a[:, t]) + mid_b, mid_r)
        act_c[:, t] = act.astype(jnp.bfloat16)
        mid_slope[:, t] = slope

    def pull_back(rows):
        fill_columns(columns, rows, True)
        for t in tiles:
            act_a[:, t] = (dot(out_turned[...], columns[:, t]) * mid_slope[:, t]).astype(jnp.bfloat16)
        for t in tiles:
            act_b[:, t] = (dot(mid_weight[...], act_a[:, t]) * in_slope[:, t]).astype(jnp.bfloat16)
        for t in tiles:
            taps[:, t] = dot(in_plain[...], act_b[:, t])
        return gather_taps(taps, width, True)

    def push(rows):
        fill_columns(columns, rows, False)
        for t in tiles:
            act_a[:, t] = (dot(in_turned[...], columns[:, t]) * in_slope[:, t]).astype(jnp.bfloat16)
        for t in tiles:
            act_b[:, t] = (dot(mid_turned[...], act_a[:, t]) * mid_slope[:, t]).astype(jnp.bfloat16)
        for t in tiles:
            taps[:, t] = dot(out_plain[...], act_b[:, t])
        return gather_taps(taps, width, False)

    def send_parts(parts, send, recv, index):
        for side in range(2):
            for r in range(2):
                send[side, CH * r : CH * (r + 1), :] = parts[2 * side + r].astype(jnp.bfloat16)
        return exchange(send, recv, index)

    def whole_rows(parts, recv, moving):
        finish(moving)
        top = inside(recv[0].astype(jnp.float32), edges_slab[0])
        bottom = inside(recv[1].astype(jnp.float32), edges_slab[1])
        return [
            inside(parts[0], edges_slab[0]) + top[:CH],
            parts[1] + top[CH:],
            parts[2] + bottom[:CH],
            inside(parts[3], edges_slab[1]) + bottom[CH:],
        ]

    def coefficient(term):
        return (-1.0) ** (term + 1) / term

    def add_term(logdet, rows, term):
        return [
            logdet[r] + coefficient(term) * jnp.sum(rows[1 + r] * signs[1 + r], axis=0, keepdims=True)
            for r in range(height)
        ]

    logdet = [jnp.zeros((1, width), jnp.float32) for _ in range(height)]

    parts = pull_back(signs)
    moving = send_parts(parts, halo_send.at[1], halo_recv.at[1], 1)
    hear_word(0)
    spread_word(1)
    for t in tiles:
        taps[:, t] = dot(out_plain[...], act_c[:, t])
    branch = gather_taps(taps, width, False)
    for r in range(height):
        lat_own_send[r] = branch[1 + r]
        lat_send[r] = branch[3 * r].astype(jnp.bfloat16)
    lat_moving = hand_over(
        (lat_send.at[0], lat_own_send, lat_send.at[1]), (lat_recv.at[1], lat_own, lat_recv.at[0]), owners, 1
    )
    pushed_1 = push(signs)
    pair_moving = send_parts(pushed_1, pair_send, pair_recv, 0)
    hear_word(1)
    spread_word(2)
    vector = whole_rows(parts, halo_recv.at[1], moving)

    parts = pull_back(vector)
    moving = send_parts(parts, halo_send.at[2], halo_recv.at[2], 2)
    logdet = add_term(logdet, vector, 1)
    take_over(lat_moving)
    outer = [inside(lat_recv[side].astype(jnp.float32), edges_own[side]) for side in range(2)]
    log_prior = []
    for r in range(height):
        whole = lat_own[r] + outer[r]
        latent = pixels[:, r, :] + (whole[:channels] + out_b)
        latent_ref[:, r, :] = latent
        log_prior.append(-0.5 * jnp.sum(latent * latent, axis=0, keepdims=True))
    pushed_2 = push(whole_rows(pushed_1, pair_recv, pair_moving))
    hear_word(2)
    vector = whole_rows(parts, halo_recv.at[2], moving)

    logdet = add_term(logdet, vector, 2)
    total = (log_prior[0] + logdet[0]) + (log_prior[1] + logdet[1])
    later = None
    for d in range(4):
        both = (coefficient(3) * pushed_1[d] + coefficient(4) * pushed_2[d]) * vector[d]
        later = both if later is None else later + both
    total = total + jnp.sum(later, axis=0, keepdims=True)
    lanes = total[:, 0:128]
    for at in range(128, width, 128):
        lanes = lanes + total[:, at : at + 128]

    def spread(value, own, slots, slot, others, sems, send_at):
        own[...] = value
        made = []
        for d, peer in enumerate(others):
            copy = pltpu.make_async_remote_copy(
                src_ref=own,
                dst_ref=slots.at[slot],
                send_sem=sum_send_sem.at[send_at + d],
                recv_sem=sems.at[slot],
                device_id={"rows": peer},
                device_id_type=MESH,
            )
            copy.start()
            made.append(copy)
        slots[slot] = value
        return made

    def collect(own, slots, slot, sems, count):
        for d in range(1, count):
            other = lax.rem(slot + d, count)
            pltpu.make_async_copy(own, slots.at[other], sems.at[other]).wait()
        value = slots[0]
        for d in range(1, count):
            value = value + slots[d]
        return value

    sums = spread(lanes, mine, group_sums, q, group_peers, group_sem, 0)

    parts = pull_back(vector)
    moving = send_parts(parts, halo_send.at[3], halo_recv.at[3], 3)
    lanes = collect(mine, group_sums, q, group_sem, group)
    sums += spread(lanes, ring_mine, ring_sums, z, ring_peers, ring_sem, group - 1)
    vector = whole_rows(parts, halo_recv.at[3], moving)

    parts = pull_back(vector)
    dots = [coefficient(4) * jnp.sum(part * sign, axis=0, keepdims=True) for part, sign in zip(parts, signs)]
    logdet = add_term(logdet, vector, 3)
    for r in range(height):
        last_send[r] = dots[3 * r]
        last_own_send[r : r + 1, :] = logdet[r] + dots[1 + r]
    moving = hand_over(
        (last_send.at[0], last_own_send, last_send.at[1]), (last_recv.at[1], last_own, last_recv.at[0]), owners, 2
    )
    take_over(moving)
    spare = [inside(last_recv[side], edges_own[side]) for side in range(2)]
    base = 8.0 + 0.5 * math.log(2.0 * math.pi) / math.log(2.0)
    rate = 1.0 / (channels * math.log(2.0))
    for r in range(height):
        bits_ref[r : r + 1, :] = base - rate * (log_prior[r] + (last_own[r : r + 1, :] + spare[r]))

    lanes = collect(ring_mine, ring_sums, z, ring_sem, ring)
    mean_ref[0] = base - jnp.sum(lanes) * (rate / (n_rows * height * width))
    for copy in sums:
        copy.wait_send()


def solution(mesh):
    n_rows = mesh.shape["rows"]
    group = min(8, n_rows // 2)
    ring = n_rows // group

    def per_device(
        pixels, probes, in_weight, in_bias, in_beta, mid_weight, mid_bias, mid_beta, out_weight, out_bias
    ):
        channels, height, width = pixels.shape
        hidden = mid_weight.shape[0]
        area = height * width
        f32, bf16 = jnp.float32, jnp.bfloat16
        vmem = pl.BlockSpec(memory_space=pltpu.VMEM)
        return pl.pallas_call(
            functools.partial(kernel, n_rows, group),
            out_shape=(
                pltpu.VMEM((channels, height, width), f32),
                pltpu.VMEM((height, width), f32),
                jax.ShapeDtypeStruct((1,), f32),
            ),
            in_specs=[pl.BlockSpec(memory_space=pltpu.HBM)] * 10,
            out_specs=(vmem, vmem, pl.BlockSpec(memory_space=pltpu.SMEM)),
            scratch_shapes=[
                pltpu.VMEM((channels, height, width), f32),
                pltpu.VMEM((channels, height, width), probes.dtype),
                pltpu.VMEM(in_weight.shape, bf16),
                pltpu.VMEM((1, hidden), f32),
                pltpu.VMEM((1, hidden), f32),
                pltpu.VMEM((hidden, hidden), bf16),
                pltpu.VMEM((1, hidden), f32),
                pltpu.VMEM((1, hidden), f32),
                pltpu.VMEM(out_weight.shape, bf16),
                pltpu.VMEM((1, channels), f32),
                pltpu.SemaphoreType.DMA((10,)),
                pltpu.VMEM((4, CH, width), f32),
                pltpu.VMEM((128, hidden), f32),
                pltpu.VMEM((256, hidden), f32),
                pltpu.VMEM((TAPS, hidden), bf16),
                pltpu.VMEM((hidden, TAPS), bf16),
                pltpu.VMEM((TAPS, hidden), bf16),
                pltpu.VMEM((hidden, TAPS), bf16),
                pltpu.VMEM((hidden, hidden), bf16),
                pltpu.VMEM((TAPS, area), bf16),
                pltpu.VMEM((hidden, area), f32),
                pltpu.VMEM((hidden, area), f32),
                pltpu.VMEM((hidden, area), bf16),
                pltpu.VMEM((hidden, area), bf16),
                pltpu.VMEM((hidden, area), bf16),
                pltpu.VMEM((TAPS, area), f32),
                pltpu.VMEM((4 * CH, width), bf16),
                pltpu.VMEM((4 * CH, width), bf16),
                pltpu.VMEM((2 * CH, width), bf16),
                pltpu.VMEM((2 * CH, width), bf16),
                pltpu.VMEM((TERMS, 2, 2 * CH, width), bf16),
                pltpu.VMEM((TERMS, 2, 2 * CH, width), bf16),
                pltpu.VMEM((2, 2 * CH, width), bf16),
                pltpu.VMEM((2, 2 * CH, width), bf16),
                pltpu.VMEM((2, CH, width), bf16),
                pltpu.VMEM((2, CH, width), bf16),
                pltpu.VMEM((2, CH, width), f32),
                pltpu.VMEM((2, CH, width), f32),
                pltpu.VMEM((2, 1, width), f32),
                pltpu.VMEM((2, 1, width), f32),
                pltpu.VMEM((2, width), f32),
                pltpu.VMEM((2, width), f32),
                pltpu.VMEM((1, 128), f32),
                pltpu.VMEM((group, 1, 128), f32),
                pltpu.VMEM((1, 128), f32),
                pltpu.VMEM((ring, 1, 128), f32),
                pltpu.SemaphoreType.DMA((TERMS, 2)),
                pltpu.SemaphoreType.DMA((TERMS, 2)),
                pltpu.SemaphoreType.DMA((3, 3)),
                pltpu.SemaphoreType.DMA((3, 3)),
                pltpu.SemaphoreType.DMA((group + ring - 2,)),
                pltpu.SemaphoreType.DMA((group,)),
                pltpu.SemaphoreType.DMA((ring,)),
                pltpu.SemaphoreType.REGULAR((3,)),
            ],
            compiler_params=pltpu.CompilerParams(
                collective_id=0, has_side_effects=True, vmem_limit_bytes=60 * 1024 * 1024
            ),
        )(
            pixels,
            probes,
            in_weight,
            in_bias[None, :],
            in_beta[None, :],
            mid_weight,
            mid_bias[None, :],
            mid_beta[None, :],
            out_weight,
            out_bias[None, :],
        )

    placed = (P("batch", "rows", None),) * 2 + (P(),) * 8
    return jax.shard_map(
        per_device,
        mesh=mesh,
        in_specs=placed,
        out_specs=(P("batch", "rows", None), P(("batch", "rows"), None), P("batch")),
        check_vma=False,
    )
```

```python
import functools
import math

import jax
import jax.numpy as jnp
from jax import lax
from jax.experimental import pallas as pl
from jax.experimental.pallas import tpu as pltpu
from jax.sharding import PartitionSpec as P

TERMS = 4
CH = 16
TAPS = 9 * CH
TILE = 256
MESH = pl.DeviceIdType.MESH


def from_left(x):
    lane = lax.broadcasted_iota(jnp.int32, x.shape, 1)
    return jnp.where(lane == 0, jnp.zeros_like(x), pltpu.roll(x, 1, 1))


def from_right(x):
    last = x.shape[1] - 1
    lane = lax.broadcasted_iota(jnp.int32, x.shape, 1)
    return jnp.where(lane == last, jnp.zeros_like(x), pltpu.roll(x, last, 1))


def fill_columns(columns, rows, flipped):
    width = rows[0].shape[1]
    for s, row in enumerate(rows):
        row = row.astype(jnp.bfloat16)
        for j in range(3):
            if j == 1:
                piece = row
            elif (j == 0) != flipped:
                piece = from_left(row)
            else:
                piece = from_right(row)
            for out_row in range(2):
                i = out_row + 2 - s if flipped else s - out_row
                if 0 <= i <= 2:
                    at = CH * (3 * i + j)
                    columns[at : at + CH, width * out_row : width * (out_row + 1)] = piece


def gather_taps(taps, width, flipped):
    def block(i, j, s):
        at = CH * (3 * i + j)
        return taps[at : at + CH, width * s : width * (s + 1)]

    result = []
    for d in range(4):
        total = None
        for j in range(3):
            part = None
            for s in range(2):
                i = d - s if flipped else s + 2 - d
                if 0 <= i <= 2:
                    value = block(i, j, s)
                    part = value if part is None else part + value
            if j != 1:
                part = from_right(part) if (j == 0) == flipped else from_left(part)
            total = part if total is None else total + part
        result.append(total)
    return result


def kernel(
    n_rows,
    group,
    pixels_hbm,
    probes_hbm,
    in_weight_hbm,
    in_bias_hbm,
    in_beta_hbm,
    mid_weight_hbm,
    mid_bias_hbm,
    mid_beta_hbm,
    out_weight_hbm,
    out_bias_hbm,
    latent_ref,
    bits_ref,
    mean_ref,
    pixels,
    probes,
    in_weight,
    in_bias,
    in_beta,
    mid_weight,
    mid_bias,
    mid_beta,
    out_weight,
    out_bias,
    load_sem,
    pad_rows,
    small_pad,
    weight_pad,
    in_plain,
    in_turned,
    out_plain,
    out_turned,
    mid_turned,
    columns,
    in_slope,
    mid_slope,
    act_a,
    act_b,
    act_c,
    taps,
    slab_send,
    slab_own,
    slab_above,
    slab_below,
    halo_send,
    halo_recv,
    pair_send,
    pair_recv,
    lat_send,
    lat_recv,
    lat_own_send,
    lat_own,
    last_send,
    last_recv,
    last_own_send,
    last_own,
    pair_mine,
    pair_sums,
    chip_mine,
    chip_sums,
    send_sem,
    recv_sem,
    three_send,
    three_recv,
    pair_sem,
    chip_sem,
    known_sem,
):
    channels, height, width = pixels.shape
    me = lax.axis_index("rows")
    ring = n_rows // group
    q = lax.rem(me, group)
    z = me // group
    group_peers = [z * group + lax.rem(q + d, group) for d in range(1, group)]
    span = group // 2
    moves = [(dz, dx) for dz in range(ring) for dx in range(span) if dz or dx]
    moves.sort(key=lambda m: -(min(m[0], ring - m[0]) + min(m[1], span - m[1])))
    chip_peers = [
        lax.rem(z + dz, ring) * group + 2 * lax.rem(q // 2 + dx, span) + lax.rem(q, 2) for dz, dx in moves
    ]

    def worker(slab):
        layer = slab // group
        s = lax.rem(slab, group)
        back = group - 1 - s
        swapped = back + 1 - 2 * lax.rem(back, 2)
        return layer * group + s + lax.rem(layer, 2) * (swapped - s)

    def step(slab, by):
        return lax.rem(slab + n_rows + by, n_rows)

    slab = worker(me)
    stays = slab == me
    owners = (step(slab, -1), slab, step(slab, 1))
    workers = (worker(step(me, -1)), slab, worker(step(me, 1)))
    up, down = worker(owners[0]), worker(owners[2])
    edges_slab = (slab == 0, slab == n_rows - 1)
    edges_own = (me == 0, me == n_rows - 1)

    sources = (
        pixels_hbm,
        probes_hbm,
        in_bias_hbm,
        in_beta_hbm,
        mid_bias_hbm,
        mid_beta_hbm,
        out_bias_hbm,
        in_weight_hbm,
        out_weight_hbm,
        mid_weight_hbm,
    )
    places = (pixels, probes, in_bias, in_beta, mid_bias, mid_beta, out_bias, in_weight, out_weight, mid_weight)
    loads = [
        pltpu.make_async_copy(source, place, load_sem.at[k]) for k, (source, place) in enumerate(zip(sources, places))
    ]
    for load in loads[:2]:
        load.start()

    def signal(sem, peer):
        pl.semaphore_signal(sem, inc=1, device_id={"rows": peer}, device_id_type=MESH)

    def around(by):
        return [lax.rem(z + d, ring) * group + q for d in (by, ring - by)]

    barrier = pltpu.get_barrier_semaphore()
    greeted = [up, down, owners[0], owners[2], workers[0], workers[2]] + group_peers + around(1) + (around(2) if ring > 2 else [])
    for peer in greeted:
        signal(barrier, peer)
    for load in loads[2:]:
        load.start()

    steps = []
    reach = 0
    while reach < ring // 2:
        steps.append(min(reach + 2, 2 * reach + 1, ring // 2 - reach))
        reach += steps[-1]

    def spread_word(k):
        if k < len(steps):
            for peer in around(steps[k]):
                signal(known_sem.at[k], peer)

    def hear_word(k):
        if k < len(steps):
            pl.semaphore_wait(known_sem.at[k], 2)

    loads[0].wait()
    loads[1].wait()
    pad_rows[...] = jnp.zeros_like(pad_rows)
    for r in range(height):
        pad_rows[2 * r, 0:channels, :] = pixels[:, r, :]
        pad_rows[2 * r + 1, 0:channels, :] = (2 * probes[:, r, :] - 1).astype(jnp.float32)
    for k in range(2 * height):
        slab_send[CH * k : CH * (k + 1), :] = pad_rows[k].astype(jnp.bfloat16)

    pl.semaphore_wait(barrier, len(greeted))

    def remote(source, place, sent, arrived, peer):
        return pltpu.make_async_remote_copy(
            src_ref=source,
            dst_ref=place,
            send_sem=sent,
            recv_sem=arrived,
            device_id={"rows": peer},
            device_id_type=MESH,
        )

    def exchange(send, recv, index):
        made = [
            remote(send.at[side], recv.at[1 - side], send_sem.at[index, side], recv_sem.at[index, 1 - side], peer)
            for side, peer in enumerate((up, down))
        ]
        for copy in made:
            copy.start()
        return made

    def finish(made):
        for copy in made:
            copy.wait()

    def hand_over(sources, places, peers, index):
        made = [
            remote(source, place, three_send.at[index, k], three_recv.at[index, k], peer)
            for k, (source, place, peer) in enumerate(zip(sources, places, peers))
        ]
        made[0].start()
        made[2].start()
        local = pltpu.make_async_copy(sources[1], places[1], three_recv.at[index, 1])

        @pl.when(jnp.logical_not(stays))
        def _():
            made[1].start()

        @pl.when(stays)
        def _():
            local.start()

        return made

    def take_over(made):
        for copy in made:
            copy.wait_recv()
        made[0].wait_send()
        made[2].wait_send()

        @pl.when(jnp.logical_not(stays))
        def _():
            made[1].wait_send()

    def inside(value, outside):
        return jnp.where(outside, 0.0, value)

    first = hand_over(
        (slab_send.at[0 : 2 * CH], slab_send, slab_send.at[2 * CH : 4 * CH]),
        (slab_below, slab_own, slab_above),
        workers,
        0,
    )
    spread_word(0)

    for load in loads[2:]:
        load.wait()
    small_pad[...] = jnp.zeros_like(small_pad)
    for k, vector_ref in enumerate((in_bias, in_beta, mid_bias, mid_beta)):
        small_pad[k : k + 1, :] = vector_ref[...]
    small_pad[4:5, 0:channels] = out_bias[...]
    small = small_pad[...].T
    in_b, in_r, mid_b, mid_r = (small[:, k : k + 1] for k in range(4))
    in_r = 0.5 * in_r
    mid_r = 0.5 * mid_r
    out_b = small[:channels, 4:5]

    weight_pad[...] = jnp.zeros_like(weight_pad)
    for source, plain, turned in ((in_weight, in_plain, in_turned), (out_weight, out_plain, out_turned)):
        for i in range(3):
            for j in range(3):
                at = CH * (3 * i + j)
                weight_pad[at : at + channels, :] = source[i, j].astype(jnp.float32)
        whole = weight_pad[...]
        plain[...] = whole[:TAPS].astype(jnp.bfloat16)
        turned[...] = whole.T[:, :TAPS].astype(jnp.bfloat16)
    mid_turned[...] = mid_weight[...].T

    take_over(first)
    above, own, below = (ref[...].astype(jnp.float32) for ref in (slab_above, slab_own, slab_below))
    pix_rows = [inside(above[:CH], edges_slab[0]), own[:CH], own[2 * CH : 3 * CH], inside(below[:CH], edges_slab[1])]
    signs = [inside(above[CH:], edges_slab[0]), own[CH : 2 * CH], own[3 * CH :], inside(below[CH:], edges_slab[1])]

    tiles = [slice(at, at + TILE) for at in range(0, height * width, TILE)]

    def dot(a, b):
        return jnp.dot(a, b, preferred_element_type=jnp.float32)

    scale = 0.5 / 1.1

    def lip(value, half_rate):
        half = half_rate * value
        t = jnp.tanh(half)
        gate = scale * (1.0 + t)
        return gate * value, gate * (1.0 + half * (1.0 - t))

    fill_columns(columns, pix_rows, False)
    def first_layer(t):
        act, slope = lip(dot(in_turned[...], columns[:, t]) + in_b, in_r)
        act_a[:, t] = act.astype(jnp.bfloat16)
        in_slope[:, t] = slope

    def second_layer(t):
        act, slope = lip(dot(mid_turned[...], act_a[:, t]) + mid_b, mid_r)
        act_c[:, t] = act.astype(jnp.bfloat16)
        mid_slope[:, t] = slope

    first_layer(tiles[0])
    for before, t in zip(tiles, tiles[1:]):
        first_layer(t)
        second_layer(before)
    second_layer(tiles[-1])

    def pull_back(rows):
        fill_columns(columns, rows, True)
        for t in tiles:
            act_a[:, t] = (dot(out_turned[...], columns[:, t]) * mid_slope[:, t]).astype(jnp.bfloat16)
        for t in tiles:
            act_b[:, t] = (dot(mid_weight[...], act_a[:, t]) * in_slope[:, t]).astype(jnp.bfloat16)
        for t in tiles:
            taps[:, t] = dot(in_plain[...], act_b[:, t])
        return gather_taps(taps, width, True)

    def push(rows):
        fill_columns(columns, rows, False)
        for t in tiles:
            act_a[:, t] = (dot(in_turned[...], columns[:, t]) * in_slope[:, t]).astype(jnp.bfloat16)
        for t in tiles:
            act_b[:, t] = (dot(mid_turned[...], act_a[:, t]) * mid_slope[:, t]).astype(jnp.bfloat16)
        for t in tiles:
            taps[:, t] = dot(out_plain[...], act_b[:, t])
        return gather_taps(taps, width, False)

    def send_parts(parts, send, recv, index):
        for side in range(2):
            for r in range(2):
                send[side, CH * r : CH * (r + 1), :] = parts[2 * side + r].astype(jnp.bfloat16)
        return exchange(send, recv, index)

    def whole_rows(parts, recv, moving):
        finish(moving)
        top = inside(recv[0].astype(jnp.float32), edges_slab[0])
        bottom = inside(recv[1].astype(jnp.float32), edges_slab[1])
        return [
            inside(parts[0], edges_slab[0]) + top[:CH],
            parts[1] + top[CH:],
            parts[2] + bottom[:CH],
            inside(parts[3], edges_slab[1]) + bottom[CH:],
        ]

    def coefficient(term):
        return (-1.0) ** (term + 1) / term

    def add_term(logdet, rows, term):
        return [
            logdet[r] + coefficient(term) * jnp.sum(rows[1 + r] * signs[1 + r], axis=0, keepdims=True)
            for r in range(height)
        ]

    logdet = [jnp.zeros((1, width), jnp.float32) for _ in range(height)]

    parts = pull_back(signs)
    moving = send_parts(parts, halo_send.at[1], halo_recv.at[1], 1)
    hear_word(0)
    spread_word(1)
    for t in tiles:
        taps[:, t] = dot(out_plain[...], act_c[:, t])
    branch = gather_taps(taps, width, False)
    for r in range(height):
        lat_own_send[r] = branch[1 + r]
        lat_send[r] = branch[3 * r].astype(jnp.bfloat16)
    lat_moving = hand_over(
        (lat_send.at[0], lat_own_send, lat_send.at[1]), (lat_recv.at[1], lat_own, lat_recv.at[0]), owners, 1
    )
    pushed_1 = push(signs)
    pair_moving = send_parts(pushed_1, pair_send, pair_recv, 0)
    hear_word(1)
    spread_word(2)
    vector = whole_rows(parts, halo_recv.at[1], moving)

    parts = pull_back(vector)
    moving = send_parts(parts, halo_send.at[2], halo_recv.at[2], 2)
    logdet = add_term(logdet, vector, 1)
    take_over(lat_moving)
    outer = [inside(lat_recv[side].astype(jnp.float32), edges_own[side]) for side in range(2)]
    log_prior = []
    for r in range(height):
        whole = lat_own[r] + outer[r]
        latent = pixels[:, r, :] + (whole[:channels] + out_b)
        latent_ref[:, r, :] = latent
        log_prior.append(-0.5 * jnp.sum(latent * latent, axis=0, keepdims=True))
    pushed_2 = push(whole_rows(pushed_1, pair_recv, pair_moving))
    hear_word(2)
    vector = whole_rows(parts, halo_recv.at[2], moving)

    logdet = add_term(logdet, vector, 2)
    total = (log_prior[0] + logdet[0]) + (log_prior[1] + logdet[1])
    later = None
    for d in range(4):
        both = (coefficient(3) * pushed_1[d] + coefficient(4) * pushed_2[d]) * vector[d]
        later = both if later is None else later + both
    total = total + jnp.sum(later, axis=0, keepdims=True)
    lanes = total[:, 0:128]
    for at in range(128, width, 128):
        lanes = lanes + total[:, at : at + 128]

    core = lax.rem(me, 2)
    chip = me // 2
    pair_mine[...] = lanes
    pair_sums[core] = lanes
    pair_copy = remote(pair_mine, pair_sums.at[core], pair_sem.at[0], pair_sem.at[1], me + 1 - 2 * core)
    pair_copy.start()


    parts = pull_back(vector)
    moving = send_parts(parts, halo_send.at[3], halo_recv.at[3], 3)
    pair_copy.wait()
    lanes = pair_sums[0] + pair_sums[1]
    chip_mine[...] = lanes
    chip_sums[chip] = lanes
    for peer in chip_peers:
        remote(chip_mine, chip_sums.at[chip], chip_sem.at[0], chip_sem.at[1], peer).start()
    vector = whole_rows(parts, halo_recv.at[3], moving)

    parts = pull_back(vector)
    dots = [coefficient(4) * jnp.sum(part * sign, axis=0, keepdims=True) for part, sign in zip(parts, signs)]
    logdet = add_term(logdet, vector, 3)
    for r in range(height):
        last_send[r] = dots[3 * r]
        last_own_send[r : r + 1, :] = logdet[r] + dots[1 + r]
    moving = hand_over(
        (last_send.at[0], last_own_send, last_send.at[1]), (last_recv.at[1], last_own, last_recv.at[0]), owners, 2
    )
    take_over(moving)
    spare = [inside(last_recv[side], edges_own[side]) for side in range(2)]
    base = 8.0 + 0.5 * math.log(2.0 * math.pi) / math.log(2.0)
    rate = 1.0 / (channels * math.log(2.0))
    for r in range(height):
        bits_ref[r : r + 1, :] = base - rate * (log_prior[r] + (last_own[r : r + 1, :] + spare[r]))

    arrived = chip_sums.at[pl.ds(0, n_rows // 2 - 1)]
    pltpu.make_async_copy(arrived, arrived, chip_sem.at[1]).wait()
    mean_ref[0] = base - jnp.sum(chip_sums[...]) * (rate / (n_rows * height * width))
    pltpu.make_async_copy(arrived, arrived, chip_sem.at[0]).wait()


def write_out(latent, bits, latent_out, bits_out, sems):
    copies = [
        pltpu.make_async_copy(latent, latent_out, sems.at[0]),
        pltpu.make_async_copy(bits, bits_out, sems.at[1]),
    ]
    for copy in copies:
        copy.start()
    for copy in copies:
        copy.wait()


def solution(mesh):
    n_rows = mesh.shape["rows"]
    group = min(8, n_rows // 2)
    ring = n_rows // group

    def per_device(
        pixels, probes, in_weight, in_bias, in_beta, mid_weight, mid_bias, mid_beta, out_weight, out_bias
    ):
        channels, height, width = pixels.shape
        hidden = mid_weight.shape[0]
        area = height * width
        f32, bf16 = jnp.float32, jnp.bfloat16
        vmem = pl.BlockSpec(memory_space=pltpu.VMEM)
        latent, bits, mean = pl.pallas_call(
            functools.partial(kernel, n_rows, group),
            out_shape=(
                pltpu.VMEM((channels, height, width), f32),
                pltpu.VMEM((height, width), f32),
                jax.ShapeDtypeStruct((1,), f32),
            ),
            in_specs=[pl.BlockSpec(memory_space=pltpu.HBM)] * 10,
            out_specs=(vmem, vmem, pl.BlockSpec(memory_space=pltpu.SMEM)),
            scratch_shapes=[
                pltpu.VMEM((channels, height, width), f32),
                pltpu.VMEM((channels, height, width), probes.dtype),
                pltpu.VMEM(in_weight.shape, bf16),
                pltpu.VMEM((1, hidden), f32),
                pltpu.VMEM((1, hidden), f32),
                pltpu.VMEM((hidden, hidden), bf16),
                pltpu.VMEM((1, hidden), f32),
                pltpu.VMEM((1, hidden), f32),
                pltpu.VMEM(out_weight.shape, bf16),
                pltpu.VMEM((1, channels), f32),
                pltpu.SemaphoreType.DMA((10,)),
                pltpu.VMEM((4, CH, width), f32),
                pltpu.VMEM((128, hidden), f32),
                pltpu.VMEM((256, hidden), f32),
                pltpu.VMEM((TAPS, hidden), bf16),
                pltpu.VMEM((hidden, TAPS), bf16),
                pltpu.VMEM((TAPS, hidden), bf16),
                pltpu.VMEM((hidden, TAPS), bf16),
                pltpu.VMEM((hidden, hidden), bf16),
                pltpu.VMEM((TAPS, area), bf16),
                pltpu.VMEM((hidden, area), f32),
                pltpu.VMEM((hidden, area), f32),
                pltpu.VMEM((hidden, area), bf16),
                pltpu.VMEM((hidden, area), bf16),
                pltpu.VMEM((hidden, area), bf16),
                pltpu.VMEM((TAPS, area), f32),
                pltpu.VMEM((4 * CH, width), bf16),
                pltpu.VMEM((4 * CH, width), bf16),
                pltpu.VMEM((2 * CH, width), bf16),
                pltpu.VMEM((2 * CH, width), bf16),
                pltpu.VMEM((TERMS, 2, 2 * CH, width), bf16),
                pltpu.VMEM((TERMS, 2, 2 * CH, width), bf16),
                pltpu.VMEM((2, 2 * CH, width), bf16),
                pltpu.VMEM((2, 2 * CH, width), bf16),
                pltpu.VMEM((2, CH, width), bf16),
                pltpu.VMEM((2, CH, width), bf16),
                pltpu.VMEM((2, CH, width), f32),
                pltpu.VMEM((2, CH, width), f32),
                pltpu.VMEM((2, 1, width), f32),
                pltpu.VMEM((2, 1, width), f32),
                pltpu.VMEM((2, width), f32),
                pltpu.VMEM((2, width), f32),
                pltpu.VMEM((1, 128), f32),
                pltpu.VMEM((2, 1, 128), f32),
                pltpu.VMEM((1, 128), f32),
                pltpu.VMEM((n_rows // 2, 1, 128), f32),
                pltpu.SemaphoreType.DMA((TERMS, 2)),
                pltpu.SemaphoreType.DMA((TERMS, 2)),
                pltpu.SemaphoreType.DMA((3, 3)),
                pltpu.SemaphoreType.DMA((3, 3)),
                pltpu.SemaphoreType.DMA((2,)),
                pltpu.SemaphoreType.DMA((2,)),
                pltpu.SemaphoreType.REGULAR((3,)),
            ],
            compiler_params=pltpu.CompilerParams(
                collective_id=0, has_side_effects=True, vmem_limit_bytes=60 * 1024 * 1024
            ),
        )(
            pixels,
            probes,
            in_weight,
            in_bias[None, :],
            in_beta[None, :],
            mid_weight,
            mid_bias[None, :],
            mid_beta[None, :],
            out_weight,
            out_bias[None, :],
        )
        hbm = pl.BlockSpec(memory_space=pltpu.HBM)
        latent, bits = pl.pallas_call(
            write_out,
            out_shape=(
                jax.ShapeDtypeStruct(latent.shape, f32),
                jax.ShapeDtypeStruct(bits.shape, f32),
            ),
            in_specs=[vmem] * 2,
            out_specs=(hbm, hbm),
            scratch_shapes=[pltpu.SemaphoreType.DMA((2,))],
            compiler_params=pltpu.CompilerParams(vmem_limit_bytes=1024 * 1024),
        )(latent, bits)
        return latent, bits, mean

    placed = (P("batch", "rows", None),) * 2 + (P(),) * 8
    return jax.shard_map(
        per_device,
        mesh=mesh,
        in_specs=placed,
        out_specs=(P("batch", "rows", None), P(("batch", "rows"), None), P("batch")),
        check_vma=False,
    )
```

```python
import functools
import math

import jax
import jax.numpy as jnp
from jax import lax
from jax.experimental import pallas as pl
from jax.experimental.pallas import tpu as pltpu
from jax.sharding import PartitionSpec as P

TERMS = 4
CH = 16
TAPS = 9 * CH
TILE = 256
BASE = 8.0 + 0.5 * math.log(2.0 * math.pi) / math.log(2.0)
MESH = pl.DeviceIdType.MESH


def from_left(x):
    lane = lax.broadcasted_iota(jnp.int32, x.shape, 1)
    return jnp.where(lane == 0, jnp.zeros_like(x), pltpu.roll(x, 1, 1))


def from_right(x):
    last = x.shape[1] - 1
    lane = lax.broadcasted_iota(jnp.int32, x.shape, 1)
    return jnp.where(lane == last, jnp.zeros_like(x), pltpu.roll(x, last, 1))


def fill_columns(columns, rows, flipped):
    width = rows[0].shape[1]
    for s, row in enumerate(rows):
        row = row.astype(jnp.bfloat16)
        for j in range(3):
            if j == 1:
                piece = row
            elif (j == 0) != flipped:
                piece = from_left(row)
            else:
                piece = from_right(row)
            for out_row in range(2):
                i = out_row + 2 - s if flipped else s - out_row
                if 0 <= i <= 2:
                    at = CH * (3 * i + j)
                    columns[at : at + CH, width * out_row : width * (out_row + 1)] = piece


def gather_taps(taps, width, flipped):
    def block(i, j, s):
        at = CH * (3 * i + j)
        return taps[at : at + CH, width * s : width * (s + 1)]

    result = []
    for d in range(4):
        total = None
        for j in range(3):
            part = None
            for s in range(2):
                i = d - s if flipped else s + 2 - d
                if 0 <= i <= 2:
                    value = block(i, j, s)
                    part = value if part is None else part + value
            if j != 1:
                part = from_right(part) if (j == 0) == flipped else from_left(part)
            total = part if total is None else total + part
        result.append(total)
    return result


def kernel(
    n_rows,
    group,
    pixels_hbm,
    probes_hbm,
    in_weight_hbm,
    in_bias_hbm,
    in_beta_hbm,
    mid_weight_hbm,
    mid_bias_hbm,
    mid_beta_hbm,
    out_weight_hbm,
    out_bias_hbm,
    latent_ref,
    bits_ref,
    sum_ref,
    pixels,
    probes,
    in_weight,
    in_bias,
    in_beta,
    mid_weight,
    mid_bias,
    mid_beta,
    out_weight,
    out_bias,
    load_sem,
    pad_rows,
    small_pad,
    weight_pad,
    in_plain,
    in_turned,
    out_plain,
    out_turned,
    mid_turned,
    columns,
    in_slope,
    mid_slope,
    act_a,
    act_b,
    act_c,
    taps,
    slab_send,
    slab_own,
    slab_above,
    slab_below,
    halo_send,
    halo_recv,
    pair_send,
    pair_recv,
    lat_send,
    lat_recv,
    lat_own_send,
    lat_own,
    last_send,
    last_recv,
    last_own_send,
    last_own,
    pair_mine,
    pair_sums,
    chip_mine,
    chip_sums,
    send_sem,
    recv_sem,
    three_send,
    three_recv,
    pair_sem,
    chip_sem,
    known_sem,
):
    channels, height, width = pixels.shape
    me = lax.axis_index("rows")
    ring = n_rows // group
    q = lax.rem(me, group)
    z = me // group
    group_peers = [z * group + lax.rem(q + d, group) for d in range(1, group)]
    span = group // 2
    moves = [(dz, dx) for dz in range(ring) for dx in range(span) if dz or dx]
    moves.sort(key=lambda m: -(min(m[0], ring - m[0]) + min(m[1], span - m[1])))
    chip_peers = [
        lax.rem(z + dz, ring) * group + 2 * lax.rem(q // 2 + dx, span) + lax.rem(q, 2) for dz, dx in moves
    ]

    def worker(slab):
        layer = slab // group
        s = lax.rem(slab, group)
        back = group - 1 - s
        swapped = back + 1 - 2 * lax.rem(back, 2)
        return layer * group + s + lax.rem(layer, 2) * (swapped - s)

    def step(slab, by):
        return lax.rem(slab + n_rows + by, n_rows)

    slab = worker(me)
    stays = slab == me
    owners = (step(slab, -1), slab, step(slab, 1))
    workers = (worker(step(me, -1)), slab, worker(step(me, 1)))
    up, down = worker(owners[0]), worker(owners[2])
    edges_slab = (slab == 0, slab == n_rows - 1)
    edges_own = (me == 0, me == n_rows - 1)

    sources = (
        pixels_hbm,
        probes_hbm,
        in_bias_hbm,
        in_beta_hbm,
        mid_bias_hbm,
        mid_beta_hbm,
        out_bias_hbm,
        in_weight_hbm,
        out_weight_hbm,
        mid_weight_hbm,
    )
    places = (pixels, probes, in_bias, in_beta, mid_bias, mid_beta, out_bias, in_weight, out_weight, mid_weight)
    loads = [
        pltpu.make_async_copy(source, place, load_sem.at[k]) for k, (source, place) in enumerate(zip(sources, places))
    ]
    for load in loads[:2]:
        load.start()

    def signal(sem, peer):
        pl.semaphore_signal(sem, inc=1, device_id={"rows": peer}, device_id_type=MESH)

    def around(by):
        return [lax.rem(z + d, ring) * group + q for d in (by, ring - by)]

    barrier = pltpu.get_barrier_semaphore()
    greeted = [up, down, owners[0], owners[2], workers[0], workers[2]] + group_peers + around(1) + (around(2) if ring > 2 else [])
    for peer in greeted:
        signal(barrier, peer)
    for load in loads[2:]:
        load.start()

    steps = []
    reach = 0
    while reach < ring // 2:
        steps.append(min(reach + 2, 2 * reach + 1, ring // 2 - reach))
        reach += steps[-1]

    def spread_word(k):
        if k < len(steps):
            for peer in around(steps[k]):
                signal(known_sem.at[k], peer)

    def hear_word(k):
        if k < len(steps):
            pl.semaphore_wait(known_sem.at[k], 2)

    loads[0].wait()
    loads[1].wait()
    pad_rows[...] = jnp.zeros_like(pad_rows)
    for r in range(height):
        pad_rows[2 * r, 0:channels, :] = pixels[:, r, :]
        pad_rows[2 * r + 1, 0:channels, :] = (2 * probes[:, r, :] - 1).astype(jnp.float32)
    for k in range(2 * height):
        slab_send[CH * k : CH * (k + 1), :] = pad_rows[k].astype(jnp.bfloat16)

    pl.semaphore_wait(barrier, len(greeted))

    def remote(source, place, sent, arrived, peer):
        return pltpu.make_async_remote_copy(
            src_ref=source,
            dst_ref=place,
            send_sem=sent,
            recv_sem=arrived,
            device_id={"rows": peer},
            device_id_type=MESH,
        )

    def exchange(send, recv, index):
        made = [
            remote(send.at[side], recv.at[1 - side], send_sem.at[index, side], recv_sem.at[index, 1 - side], peer)
            for side, peer in enumerate((up, down))
        ]
        for copy in made:
            copy.start()
        return made

    def finish(made):
        for copy in made:
            copy.wait()

    def hand_over(sources, places, peers, index):
        made = [
            remote(source, place, three_send.at[index, k], three_recv.at[index, k], peer)
            for k, (source, place, peer) in enumerate(zip(sources, places, peers))
        ]
        made[0].start()
        made[2].start()
        local = pltpu.make_async_copy(sources[1], places[1], three_recv.at[index, 1])

        @pl.when(jnp.logical_not(stays))
        def _():
            made[1].start()

        @pl.when(stays)
        def _():
            local.start()

        return made

    def take_over(made):
        for copy in made:
            copy.wait_recv()
        made[0].wait_send()
        made[2].wait_send()

        @pl.when(jnp.logical_not(stays))
        def _():
            made[1].wait_send()

    def inside(value, outside):
        return jnp.where(outside, 0.0, value)

    first = hand_over(
        (slab_send.at[0 : 2 * CH], slab_send, slab_send.at[2 * CH : 4 * CH]),
        (slab_below, slab_own, slab_above),
        workers,
        0,
    )
    spread_word(0)

    for load in loads[2:]:
        load.wait()
    small_pad[...] = jnp.zeros_like(small_pad)
    for k, vector_ref in enumerate((in_bias, in_beta, mid_bias, mid_beta)):
        small_pad[k : k + 1, :] = vector_ref[...]
    small_pad[4:5, 0:channels] = out_bias[...]
    small = small_pad[...].T
    in_b, in_r, mid_b, mid_r = (small[:, k : k + 1] for k in range(4))
    in_r = 0.5 * in_r
    mid_r = 0.5 * mid_r
    out_b = small[:channels, 4:5]

    weight_pad[...] = jnp.zeros_like(weight_pad)
    for source, plain, turned in ((in_weight, in_plain, in_turned), (out_weight, out_plain, out_turned)):
        for i in range(3):
            for j in range(3):
                at = CH * (3 * i + j)
                weight_pad[at : at + channels, :] = source[i, j].astype(jnp.float32)
        whole = weight_pad[...]
        plain[...] = whole[:TAPS].astype(jnp.bfloat16)
        turned[...] = whole.T[:, :TAPS].astype(jnp.bfloat16)
    mid_turned[...] = mid_weight[...].T

    take_over(first)
    above, own, below = (ref[...].astype(jnp.float32) for ref in (slab_above, slab_own, slab_below))
    pix_rows = [inside(above[:CH], edges_slab[0]), own[:CH], own[2 * CH : 3 * CH], inside(below[:CH], edges_slab[1])]
    signs = [inside(above[CH:], edges_slab[0]), own[CH : 2 * CH], own[3 * CH :], inside(below[CH:], edges_slab[1])]

    tiles = [slice(at, at + TILE) for at in range(0, height * width, TILE)]

    def dot(a, b):
        return jnp.dot(a, b, preferred_element_type=jnp.float32)

    scale = 0.5 / 1.1

    def lip(value, half_rate):
        half = half_rate * value
        t = jnp.tanh(half)
        gate = scale * (1.0 + t)
        return gate * value, gate * (1.0 + half * (1.0 - t))

    fill_columns(columns, pix_rows, False)
    def first_layer(t):
        act, slope = lip(dot(in_turned[...], columns[:, t]) + in_b, in_r)
        act_a[:, t] = act.astype(jnp.bfloat16)
        in_slope[:, t] = slope

    def second_layer(t):
        act, slope = lip(dot(mid_turned[...], act_a[:, t]) + mid_b, mid_r)
        act_c[:, t] = act.astype(jnp.bfloat16)
        mid_slope[:, t] = slope

    first_layer(tiles[0])
    for before, t in zip(tiles, tiles[1:]):
        first_layer(t)
        second_layer(before)
    second_layer(tiles[-1])

    def pull_back(rows, between=None):
        fill_columns(columns, rows, True)
        for t in tiles:
            act_a[:, t] = (dot(out_turned[...], columns[:, t]) * mid_slope[:, t]).astype(jnp.bfloat16)
        for t in tiles:
            act_b[:, t] = (dot(mid_weight[...], act_a[:, t]) * in_slope[:, t]).astype(jnp.bfloat16)
        if between is not None:
            between()
        for t in tiles:
            taps[:, t] = dot(in_plain[...], act_b[:, t])
        return gather_taps(taps, width, True)

    def push(rows):
        fill_columns(columns, rows, False)
        for t in tiles:
            act_a[:, t] = (dot(in_turned[...], columns[:, t]) * in_slope[:, t]).astype(jnp.bfloat16)
        for t in tiles:
            act_b[:, t] = (dot(mid_turned[...], act_a[:, t]) * mid_slope[:, t]).astype(jnp.bfloat16)
        for t in tiles:
            taps[:, t] = dot(out_plain[...], act_b[:, t])
        return gather_taps(taps, width, False)

    def send_parts(parts, send, recv, index):
        for side in range(2):
            for r in range(2):
                send[side, CH * r : CH * (r + 1), :] = parts[2 * side + r].astype(jnp.bfloat16)
        return exchange(send, recv, index)

    def whole_rows(parts, recv, moving):
        finish(moving)
        top = inside(recv[0].astype(jnp.float32), edges_slab[0])
        bottom = inside(recv[1].astype(jnp.float32), edges_slab[1])
        return [
            inside(parts[0], edges_slab[0]) + top[:CH],
            parts[1] + top[CH:],
            parts[2] + bottom[:CH],
            inside(parts[3], edges_slab[1]) + bottom[CH:],
        ]

    def coefficient(term):
        return (-1.0) ** (term + 1) / term

    def add_term(logdet, rows, term):
        return [
            logdet[r] + coefficient(term) * jnp.sum(rows[1 + r] * signs[1 + r], axis=0, keepdims=True)
            for r in range(height)
        ]

    logdet = [jnp.zeros((1, width), jnp.float32) for _ in range(height)]

    parts = pull_back(signs)
    moving = send_parts(parts, halo_send.at[1], halo_recv.at[1], 1)
    hear_word(0)
    spread_word(1)
    for t in tiles:
        taps[:, t] = dot(out_plain[...], act_c[:, t])
    branch = gather_taps(taps, width, False)
    for r in range(height):
        lat_own_send[r] = branch[1 + r]
        lat_send[r] = branch[3 * r].astype(jnp.bfloat16)
    lat_moving = hand_over(
        (lat_send.at[0], lat_own_send, lat_send.at[1]), (lat_recv.at[1], lat_own, lat_recv.at[0]), owners, 1
    )
    pushed_1 = push(signs)
    pair_moving = send_parts(pushed_1, pair_send, pair_recv, 0)
    hear_word(1)
    spread_word(2)
    vector = whole_rows(parts, halo_recv.at[1], moving)

    parts = pull_back(vector)
    moving = send_parts(parts, halo_send.at[2], halo_recv.at[2], 2)
    logdet = add_term(logdet, vector, 1)
    take_over(lat_moving)
    outer = [inside(lat_recv[side].astype(jnp.float32), edges_own[side]) for side in range(2)]
    log_prior = []
    for r in range(height):
        whole = lat_own[r] + outer[r]
        latent = pixels[:, r, :] + (whole[:channels] + out_b)
        latent_ref[:, r, :] = latent
        log_prior.append(-0.5 * jnp.sum(latent * latent, axis=0, keepdims=True))
    pushed_2 = push(whole_rows(pushed_1, pair_recv, pair_moving))
    hear_word(2)
    vector = whole_rows(parts, halo_recv.at[2], moving)

    logdet = add_term(logdet, vector, 2)
    total = (log_prior[0] + logdet[0]) + (log_prior[1] + logdet[1])
    later = None
    for d in range(4):
        both = (coefficient(3) * pushed_1[d] + coefficient(4) * pushed_2[d]) * vector[d]
        later = both if later is None else later + both
    total = total + jnp.sum(later, axis=0, keepdims=True)
    lanes = total[:, 0:128]
    for at in range(128, width, 128):
        lanes = lanes + total[:, at : at + 128]

    core = lax.rem(me, 2)
    chip = me // 2
    pair_mine[...] = lanes
    pair_sums[core] = lanes
    pair_copy = remote(pair_mine, pair_sums.at[core], pair_sem.at[0], pair_sem.at[1], me + 1 - 2 * core)
    pair_copy.start()


    def spread_sum():
        pair_copy.wait()
        lanes = pair_sums[0] + pair_sums[1]
        chip_mine[...] = lanes
        chip_sums[chip] = lanes
        for peer in chip_peers:
            remote(chip_mine, chip_sums.at[chip], chip_sem.at[0], chip_sem.at[1], peer).start()

    parts = pull_back(vector, spread_sum)
    moving = send_parts(parts, halo_send.at[3], halo_recv.at[3], 3)
    vector = whole_rows(parts, halo_recv.at[3], moving)

    parts = pull_back(vector)
    dots = [coefficient(4) * jnp.sum(part * sign, axis=0, keepdims=True) for part, sign in zip(parts, signs)]
    logdet = add_term(logdet, vector, 3)
    for r in range(height):
        last_send[r] = dots[3 * r]
        last_own_send[r : r + 1, :] = logdet[r] + dots[1 + r]
    moving = hand_over(
        (last_send.at[0], last_own_send, last_send.at[1]), (last_recv.at[1], last_own, last_recv.at[0]), owners, 2
    )
    take_over(moving)
    spare = [inside(last_recv[side], edges_own[side]) for side in range(2)]
    rate = 1.0 / (channels * math.log(2.0))
    for r in range(height):
        bits_ref[r : r + 1, :] = BASE - rate * (log_prior[r] + (last_own[r : r + 1, :] + spare[r]))

    arrived = chip_sums.at[pl.ds(0, n_rows // 2 - 1)]
    pltpu.make_async_copy(arrived, arrived, chip_sem.at[1]).wait()
    sum_ref[...] = jnp.sum(chip_sums[...], axis=0)
    pltpu.make_async_copy(arrived, arrived, chip_sem.at[0]).wait()


def write_out(rate, latent, bits, sums, latent_out, bits_out, mean_out, mean, sems):
    copies = [
        pltpu.make_async_copy(latent, latent_out, sems.at[0]),
        pltpu.make_async_copy(bits, bits_out, sems.at[1]),
    ]
    for copy in copies:
        copy.start()
    mean[0] = BASE - jnp.sum(sums[...]) * rate
    copies.append(pltpu.make_async_copy(mean, mean_out, sems.at[2]))
    copies[2].start()
    for copy in copies:
        copy.wait()


def solution(mesh):
    n_rows = mesh.shape["rows"]
    group = min(8, n_rows // 2)
    ring = n_rows // group

    def per_device(
        pixels, probes, in_weight, in_bias, in_beta, mid_weight, mid_bias, mid_beta, out_weight, out_bias
    ):
        channels, height, width = pixels.shape
        hidden = mid_weight.shape[0]
        area = height * width
        f32, bf16 = jnp.float32, jnp.bfloat16
        vmem = pl.BlockSpec(memory_space=pltpu.VMEM)
        latent, bits, sums = pl.pallas_call(
            functools.partial(kernel, n_rows, group),
            out_shape=(
                pltpu.VMEM((channels, height, width), f32),
                pltpu.VMEM((height, width), f32),
                pltpu.VMEM((1, 128), f32),
            ),
            in_specs=[pl.BlockSpec(memory_space=pltpu.HBM)] * 10,
            out_specs=(vmem, vmem, vmem),
            scratch_shapes=[
                pltpu.VMEM((channels, height, width), f32),
                pltpu.VMEM((channels, height, width), probes.dtype),
                pltpu.VMEM(in_weight.shape, bf16),
                pltpu.VMEM((1, hidden), f32),
                pltpu.VMEM((1, hidden), f32),
                pltpu.VMEM((hidden, hidden), bf16),
                pltpu.VMEM((1, hidden), f32),
                pltpu.VMEM((1, hidden), f32),
                pltpu.VMEM(out_weight.shape, bf16),
                pltpu.VMEM((1, channels), f32),
                pltpu.SemaphoreType.DMA((10,)),
                pltpu.VMEM((4, CH, width), f32),
                pltpu.VMEM((128, hidden), f32),
                pltpu.VMEM((256, hidden), f32),
                pltpu.VMEM((TAPS, hidden), bf16),
                pltpu.VMEM((hidden, TAPS), bf16),
                pltpu.VMEM((TAPS, hidden), bf16),
                pltpu.VMEM((hidden, TAPS), bf16),
                pltpu.VMEM((hidden, hidden), bf16),
                pltpu.VMEM((TAPS, area), bf16),
                pltpu.VMEM((hidden, area), f32),
                pltpu.VMEM((hidden, area), f32),
                pltpu.VMEM((hidden, area), bf16),
                pltpu.VMEM((hidden, area), bf16),
                pltpu.VMEM((hidden, area), bf16),
                pltpu.VMEM((TAPS, area), f32),
                pltpu.VMEM((4 * CH, width), bf16),
                pltpu.VMEM((4 * CH, width), bf16),
                pltpu.VMEM((2 * CH, width), bf16),
                pltpu.VMEM((2 * CH, width), bf16),
                pltpu.VMEM((TERMS, 2, 2 * CH, width), bf16),
                pltpu.VMEM((TERMS, 2, 2 * CH, width), bf16),
                pltpu.VMEM((2, 2 * CH, width), bf16),
                pltpu.VMEM((2, 2 * CH, width), bf16),
                pltpu.VMEM((2, CH, width), bf16),
                pltpu.VMEM((2, CH, width), bf16),
                pltpu.VMEM((2, CH, width), f32),
                pltpu.VMEM((2, CH, width), f32),
                pltpu.VMEM((2, 1, width), f32),
                pltpu.VMEM((2, 1, width), f32),
                pltpu.VMEM((2, width), f32),
                pltpu.VMEM((2, width), f32),
                pltpu.VMEM((1, 128), f32),
                pltpu.VMEM((2, 1, 128), f32),
                pltpu.VMEM((1, 128), f32),
                pltpu.VMEM((n_rows // 2, 1, 128), f32),
                pltpu.SemaphoreType.DMA((TERMS, 2)),
                pltpu.SemaphoreType.DMA((TERMS, 2)),
                pltpu.SemaphoreType.DMA((3, 3)),
                pltpu.SemaphoreType.DMA((3, 3)),
                pltpu.SemaphoreType.DMA((2,)),
                pltpu.SemaphoreType.DMA((2,)),
                pltpu.SemaphoreType.REGULAR((3,)),
            ],
            compiler_params=pltpu.CompilerParams(
                collective_id=0, has_side_effects=True, vmem_limit_bytes=60 * 1024 * 1024
            ),
        )(
            pixels,
            probes,
            in_weight,
            in_bias[None, :],
            in_beta[None, :],
            mid_weight,
            mid_bias[None, :],
            mid_beta[None, :],
            out_weight,
            out_bias[None, :],
        )
        hbm = pl.BlockSpec(memory_space=pltpu.HBM)
        rate = 1.0 / (channels * math.log(2.0) * n_rows * area)
        return pl.pallas_call(
            functools.partial(write_out, rate),
            out_shape=(
                jax.ShapeDtypeStruct(latent.shape, f32),
                jax.ShapeDtypeStruct(bits.shape, f32),
                jax.ShapeDtypeStruct((1,), f32),
            ),
            in_specs=[vmem] * 3,
            out_specs=(hbm, hbm, hbm),
            scratch_shapes=[pltpu.SMEM((1,), f32), pltpu.SemaphoreType.DMA((3,))],
            compiler_params=pltpu.CompilerParams(vmem_limit_bytes=1024 * 1024),
        )(latent, bits, sums)

    placed = (P("batch", "rows", None),) * 2 + (P(),) * 8
    return jax.shard_map(
        per_device,
        mesh=mesh,
        in_specs=placed,
        out_specs=(P("batch", "rows", None), P(("batch", "rows"), None), P("batch")),
        check_vma=False,
    )
```

```python
import functools
import math

import jax
import jax.numpy as jnp
from jax import lax
from jax.experimental import pallas as pl
from jax.experimental.pallas import tpu as pltpu
from jax.sharding import PartitionSpec as P

TERMS = 4
CH = 16
TAPS = 9 * CH
TILE = 256
BASE = 8.0 + 0.5 * math.log(2.0 * math.pi) / math.log(2.0)
MESH = pl.DeviceIdType.MESH


def from_left(x):
    lane = lax.broadcasted_iota(jnp.int32, x.shape, 1)
    return jnp.where(lane == 0, jnp.zeros_like(x), pltpu.roll(x, 1, 1))


def from_right(x):
    last = x.shape[1] - 1
    lane = lax.broadcasted_iota(jnp.int32, x.shape, 1)
    return jnp.where(lane == last, jnp.zeros_like(x), pltpu.roll(x, last, 1))


def fill_columns(columns, rows, flipped):
    width = rows[0].shape[1]
    for s, row in enumerate(rows):
        row = row.astype(jnp.bfloat16)
        for j in range(3):
            if j == 1:
                piece = row
            elif (j == 0) != flipped:
                piece = from_left(row)
            else:
                piece = from_right(row)
            for out_row in range(2):
                i = out_row + 2 - s if flipped else s - out_row
                if 0 <= i <= 2:
                    at = CH * (3 * i + j)
                    columns[at : at + CH, width * out_row : width * (out_row + 1)] = piece


def gather_taps(taps, width, flipped):
    def block(i, j, s):
        at = CH * (3 * i + j)
        return taps[at : at + CH, width * s : width * (s + 1)]

    result = []
    for d in range(4):
        total = None
        for j in range(3):
            part = None
            for s in range(2):
                i = d - s if flipped else s + 2 - d
                if 0 <= i <= 2:
                    value = block(i, j, s)
                    part = value if part is None else part + value
            if j != 1:
                part = from_right(part) if (j == 0) == flipped else from_left(part)
            total = part if total is None else total + part
        result.append(total)
    return result


def kernel(
    n_rows,
    group,
    pixels_hbm,
    probes_hbm,
    in_weight_hbm,
    in_bias_hbm,
    in_beta_hbm,
    mid_weight_hbm,
    mid_bias_hbm,
    mid_beta_hbm,
    out_weight_hbm,
    out_bias_hbm,
    latent_ref,
    bits_ref,
    sum_ref,
    pixels,
    probes,
    in_weight,
    in_bias,
    in_beta,
    mid_weight,
    mid_bias,
    mid_beta,
    out_weight,
    out_bias,
    load_sem,
    pad_rows,
    small_pad,
    weight_pad,
    in_plain,
    in_turned,
    out_plain,
    out_turned,
    mid_turned,
    columns,
    in_slope,
    mid_slope,
    act_a,
    act_b,
    act_c,
    taps,
    slab_send,
    slab_own,
    slab_above,
    slab_below,
    halo_send,
    halo_recv,
    pair_send,
    pair_recv,
    lat_send,
    lat_recv,
    lat_own_send,
    lat_own,
    last_send,
    last_recv,
    last_own_send,
    last_own,
    pair_mine,
    pair_sums,
    chip_mine,
    chip_sums,
    send_sem,
    recv_sem,
    three_send,
    three_recv,
    pair_sem,
    chip_sem,
    known_sem,
):
    channels, height, width = pixels.shape
    me = lax.axis_index("rows")
    ring = n_rows // group
    q = lax.rem(me, group)
    z = me // group
    group_peers = [z * group + lax.rem(q + d, group) for d in range(1, group)]
    span = group // 2
    moves = [(dz, dx) for dz in range(ring) for dx in range(span) if dz or dx]
    moves.sort(key=lambda m: -(min(m[0], ring - m[0]) + min(m[1], span - m[1])))
    chip_peers = [
        lax.rem(z + dz, ring) * group + 2 * lax.rem(q // 2 + dx, span) + lax.rem(q, 2) for dz, dx in moves
    ]

    def worker(slab):
        layer = slab // group
        s = lax.rem(slab, group)
        back = group - 1 - s
        swapped = back + 1 - 2 * lax.rem(back, 2)
        return layer * group + s + lax.rem(layer, 2) * (swapped - s)

    def step(slab, by):
        return lax.rem(slab + n_rows + by, n_rows)

    slab = worker(me)
    stays = slab == me
    owners = (step(slab, -1), slab, step(slab, 1))
    workers = (worker(step(me, -1)), slab, worker(step(me, 1)))
    up, down = worker(owners[0]), worker(owners[2])
    edges_slab = (slab == 0, slab == n_rows - 1)
    edges_own = (me == 0, me == n_rows - 1)

    sources = (
        pixels_hbm,
        probes_hbm,
        in_bias_hbm,
        in_beta_hbm,
        mid_bias_hbm,
        mid_beta_hbm,
        out_bias_hbm,
        in_weight_hbm,
        out_weight_hbm,
        mid_weight_hbm,
    )
    places = (pixels, probes, in_bias, in_beta, mid_bias, mid_beta, out_bias, in_weight, out_weight, mid_weight)
    loads = [
        pltpu.make_async_copy(source, place, load_sem.at[k]) for k, (source, place) in enumerate(zip(sources, places))
    ]
    for load in loads[:2]:
        load.start()

    def signal(sem, peer):
        pl.semaphore_signal(sem, inc=1, device_id={"rows": peer}, device_id_type=MESH)

    def around(by):
        return [lax.rem(z + d, ring) * group + q for d in (by, ring - by)]

    barrier = pltpu.get_barrier_semaphore()
    greeted = [up, down, owners[0], owners[2], workers[0], workers[2]] + group_peers + around(1) + (around(2) if ring > 2 else [])
    for peer in greeted:
        signal(barrier, peer)
    for load in loads[2:]:
        load.start()

    steps = []
    reach = 0
    while reach < ring // 2:
        steps.append(min(reach + 2, 2 * reach + 1, ring // 2 - reach))
        reach += steps[-1]

    def spread_word(k):
        if k < len(steps):
            for peer in around(steps[k]):
                signal(known_sem.at[k], peer)

    def hear_word(k):
        if k < len(steps):
            pl.semaphore_wait(known_sem.at[k], 2)

    loads[0].wait()
    loads[1].wait()
    pad_rows[...] = jnp.zeros_like(pad_rows)
    for r in range(height):
        pad_rows[2 * r, 0:channels, :] = pixels[:, r, :]
        pad_rows[2 * r + 1, 0:channels, :] = (2 * probes[:, r, :] - 1).astype(jnp.float32)
    for k in range(2 * height):
        slab_send[CH * k : CH * (k + 1), :] = pad_rows[k].astype(jnp.bfloat16)

    pl.semaphore_wait(barrier, len(greeted))

    def remote(source, place, sent, arrived, peer):
        return pltpu.make_async_remote_copy(
            src_ref=source,
            dst_ref=place,
            send_sem=sent,
            recv_sem=arrived,
            device_id={"rows": peer},
            device_id_type=MESH,
        )

    def exchange(send, recv, index):
        made = [
            remote(send.at[side], recv.at[1 - side], send_sem.at[index, side], recv_sem.at[index, 1 - side], peer)
            for side, peer in enumerate((up, down))
        ]
        for copy in made:
            copy.start()
        return made

    def finish(made):
        for copy in made:
            copy.wait()

    def hand_over(sources, places, peers, index):
        made = [
            remote(source, place, three_send.at[index, k], three_recv.at[index, k], peer)
            for k, (source, place, peer) in enumerate(zip(sources, places, peers))
        ]
        made[0].start()
        made[2].start()
        local = pltpu.make_async_copy(sources[1], places[1], three_recv.at[index, 1])

        @pl.when(jnp.logical_not(stays))
        def _():
            made[1].start()

        @pl.when(stays)
        def _():
            local.start()

        return made

    def take_over(made):
        for copy in made:
            copy.wait_recv()
        made[0].wait_send()
        made[2].wait_send()

        @pl.when(jnp.logical_not(stays))
        def _():
            made[1].wait_send()

    def inside(value, outside):
        return jnp.where(outside, 0.0, value)

    first = hand_over(
        (slab_send.at[0 : 2 * CH], slab_send, slab_send.at[2 * CH : 4 * CH]),
        (slab_below, slab_own, slab_above),
        workers,
        0,
    )
    spread_word(0)

    for load in loads[2:]:
        load.wait()
    small_pad[...] = jnp.zeros_like(small_pad)
    for k, vector_ref in enumerate((in_bias, in_beta, mid_bias, mid_beta)):
        small_pad[k : k + 1, :] = vector_ref[...]
    small_pad[4:5, 0:channels] = out_bias[...]
    small = small_pad[...].T
    in_b, in_r, mid_b, mid_r = (small[:, k : k + 1] for k in range(4))
    in_r = 0.5 * in_r
    mid_r = 0.5 * mid_r
    out_b = small[:channels, 4:5]

    weight_pad[...] = jnp.zeros_like(weight_pad)
    for source, plain, turned in ((in_weight, in_plain, in_turned), (out_weight, out_plain, out_turned)):
        for i in range(3):
            for j in range(3):
                at = CH * (3 * i + j)
                weight_pad[at : at + channels, :] = source[i, j].astype(jnp.float32)
        whole = weight_pad[...]
        plain[...] = whole[:TAPS].astype(jnp.bfloat16)
        turned[...] = whole.T[:, :TAPS].astype(jnp.bfloat16)
    mid_turned[...] = mid_weight[...].T

    take_over(first)
    above, own, below = (ref[...].astype(jnp.float32) for ref in (slab_above, slab_own, slab_below))
    pix_rows = [inside(above[:CH], edges_slab[0]), own[:CH], own[2 * CH : 3 * CH], inside(below[:CH], edges_slab[1])]
    signs = [inside(above[CH:], edges_slab[0]), own[CH : 2 * CH], own[3 * CH :], inside(below[CH:], edges_slab[1])]

    tiles = [slice(at, at + TILE) for at in range(0, height * width, TILE)]

    def dot(a, b):
        return jnp.dot(a, b, preferred_element_type=jnp.float32)

    scale = 0.5 / 1.1

    def lip(value, half_rate):
        half = half_rate * value
        t = jnp.tanh(half)
        gate = scale * (1.0 + t)
        return gate * value, gate * (1.0 + half * (1.0 - t))

    fill_columns(columns, pix_rows, False)
    def first_layer(t):
        act, slope = lip(dot(in_turned[...], columns[:, t]) + in_b, in_r)
        act_a[:, t] = act.astype(jnp.bfloat16)
        in_slope[:, t] = slope

    def second_layer(t):
        act, slope = lip(dot(mid_turned[...], act_a[:, t]) + mid_b, mid_r)
        act_c[:, t] = act.astype(jnp.bfloat16)
        mid_slope[:, t] = slope

    first_layer(tiles[0])
    for before, t in zip(tiles, tiles[1:]):
        first_layer(t)
        second_layer(before)
    second_layer(tiles[-1])

    def pull_back(rows, between=None):
        fill_columns(columns, rows, True)
        for t in tiles:
            act_a[:, t] = (dot(out_turned[...], columns[:, t]) * mid_slope[:, t]).astype(jnp.bfloat16)
        for t in tiles:
            act_b[:, t] = (dot(mid_weight[...], act_a[:, t]) * in_slope[:, t]).astype(jnp.bfloat16)
        if between is not None:
            between()
        for t in tiles:
            taps[:, t] = dot(in_plain[...], act_b[:, t])
        return gather_taps(taps, width, True)

    def push(rows):
        fill_columns(columns, rows, False)
        for t in tiles:
            act_a[:, t] = (dot(in_turned[...], columns[:, t]) * in_slope[:, t]).astype(jnp.bfloat16)
        for t in tiles:
            act_b[:, t] = (dot(mid_turned[...], act_a[:, t]) * mid_slope[:, t]).astype(jnp.bfloat16)
        for t in tiles:
            taps[:, t] = dot(out_plain[...], act_b[:, t])
        return gather_taps(taps, width, False)

    def send_parts(parts, send, recv, index):
        for side in range(2):
            for r in range(2):
                send[side, CH * r : CH * (r + 1), :] = parts[2 * side + r].astype(jnp.bfloat16)
        return exchange(send, recv, index)

    def whole_rows(parts, recv, moving):
        finish(moving)
        top = inside(recv[0].astype(jnp.float32), edges_slab[0])
        bottom = inside(recv[1].astype(jnp.float32), edges_slab[1])
        return [
            inside(parts[0], edges_slab[0]) + top[:CH],
            parts[1] + top[CH:],
            parts[2] + bottom[:CH],
            inside(parts[3], edges_slab[1]) + bottom[CH:],
        ]

    def coefficient(term):
        return (-1.0) ** (term + 1) / term

    def add_term(logdet, rows, term):
        return [
            logdet[r] + coefficient(term) * jnp.sum(rows[1 + r] * signs[1 + r], axis=0, keepdims=True)
            for r in range(height)
        ]

    logdet = [jnp.zeros((1, width), jnp.float32) for _ in range(height)]

    parts = pull_back(signs)
    moving = send_parts(parts, halo_send.at[1], halo_recv.at[1], 1)
    hear_word(0)
    spread_word(1)
    pushed_1 = push(signs)
    pair_moving = send_parts(pushed_1, pair_send, pair_recv, 0)
    for t in tiles:
        taps[:, t] = dot(out_plain[...], act_c[:, t])
    branch = gather_taps(taps, width, False)
    for r in range(height):
        lat_own_send[r] = branch[1 + r]
        lat_send[r] = branch[3 * r].astype(jnp.bfloat16)
    lat_moving = hand_over(
        (lat_send.at[0], lat_own_send, lat_send.at[1]), (lat_recv.at[1], lat_own, lat_recv.at[0]), owners, 1
    )
    hear_word(1)
    spread_word(2)
    vector = whole_rows(parts, halo_recv.at[1], moving)

    parts = pull_back(vector)
    moving = send_parts(parts, halo_send.at[2], halo_recv.at[2], 2)
    logdet = add_term(logdet, vector, 1)
    pushed_2 = push(whole_rows(pushed_1, pair_recv, pair_moving))
    take_over(lat_moving)
    outer = [inside(lat_recv[side].astype(jnp.float32), edges_own[side]) for side in range(2)]
    log_prior = []
    for r in range(height):
        whole = lat_own[r] + outer[r]
        latent = pixels[:, r, :] + (whole[:channels] + out_b)
        latent_ref[:, r, :] = latent
        log_prior.append(-0.5 * jnp.sum(latent * latent, axis=0, keepdims=True))
    hear_word(2)
    vector = whole_rows(parts, halo_recv.at[2], moving)

    logdet = add_term(logdet, vector, 2)
    total = (log_prior[0] + logdet[0]) + (log_prior[1] + logdet[1])
    later = None
    for d in range(4):
        both = (coefficient(3) * pushed_1[d] + coefficient(4) * pushed_2[d]) * vector[d]
        later = both if later is None else later + both
    total = total + jnp.sum(later, axis=0, keepdims=True)
    lanes = total[:, 0:128]
    for at in range(128, width, 128):
        lanes = lanes + total[:, at : at + 128]

    core = lax.rem(me, 2)
    chip = me // 2
    pair_mine[...] = lanes
    pair_sums[core] = lanes
    pair_copy = remote(pair_mine, pair_sums.at[core], pair_sem.at[0], pair_sem.at[1], me + 1 - 2 * core)
    pair_copy.start()


    def spread_sum():
        pair_copy.wait()
        lanes = pair_sums[0] + pair_sums[1]
        chip_mine[...] = lanes
        chip_sums[chip] = lanes
        for peer in chip_peers:
            remote(chip_mine, chip_sums.at[chip], chip_sem.at[0], chip_sem.at[1], peer).start()

    parts = pull_back(vector, spread_sum)
    moving = send_parts(parts, halo_send.at[3], halo_recv.at[3], 3)
    vector = whole_rows(parts, halo_recv.at[3], moving)

    parts = pull_back(vector)
    dots = [coefficient(4) * jnp.sum(part * sign, axis=0, keepdims=True) for part, sign in zip(parts, signs)]
    logdet = add_term(logdet, vector, 3)
    for r in range(height):
        last_send[r] = dots[3 * r]
        last_own_send[r : r + 1, :] = logdet[r] + dots[1 + r]
    moving = hand_over(
        (last_send.at[0], last_own_send, last_send.at[1]), (last_recv.at[1], last_own, last_recv.at[0]), owners, 2
    )
    take_over(moving)
    spare = [inside(last_recv[side], edges_own[side]) for side in range(2)]
    rate = 1.0 / (channels * math.log(2.0))
    for r in range(height):
        bits_ref[r : r + 1, :] = BASE - rate * (log_prior[r] + (last_own[r : r + 1, :] + spare[r]))

    arrived = chip_sums.at[pl.ds(0, n_rows // 2 - 1)]
    pltpu.make_async_copy(arrived, arrived, chip_sem.at[1]).wait()
    sum_ref[...] = jnp.sum(chip_sums[...], axis=0)
    pltpu.make_async_copy(arrived, arrived, chip_sem.at[0]).wait()


def write_out(rate, latent, bits, sums, latent_out, bits_out, mean_out, mean, sems):
    copies = [
        pltpu.make_async_copy(latent, latent_out, sems.at[0]),
        pltpu.make_async_copy(bits, bits_out, sems.at[1]),
    ]
    for copy in copies:
        copy.start()
    mean[0] = BASE - jnp.sum(sums[...]) * rate
    copies.append(pltpu.make_async_copy(mean, mean_out, sems.at[2]))
    copies[2].start()
    for copy in copies:
        copy.wait()


def solution(mesh):
    n_rows = mesh.shape["rows"]
    group = min(8, n_rows // 2)
    ring = n_rows // group

    def per_device(
        pixels, probes, in_weight, in_bias, in_beta, mid_weight, mid_bias, mid_beta, out_weight, out_bias
    ):
        channels, height, width = pixels.shape
        hidden = mid_weight.shape[0]
        area = height * width
        f32, bf16 = jnp.float32, jnp.bfloat16
        vmem = pl.BlockSpec(memory_space=pltpu.VMEM)
        latent, bits, sums = pl.pallas_call(
            functools.partial(kernel, n_rows, group),
            out_shape=(
                pltpu.VMEM((channels, height, width), f32),
                pltpu.VMEM((height, width), f32),
                pltpu.VMEM((1, 128), f32),
            ),
            in_specs=[pl.BlockSpec(memory_space=pltpu.HBM)] * 10,
            out_specs=(vmem, vmem, vmem),
            scratch_shapes=[
                pltpu.VMEM((channels, height, width), f32),
                pltpu.VMEM((channels, height, width), probes.dtype),
                pltpu.VMEM(in_weight.shape, bf16),
                pltpu.VMEM((1, hidden), f32),
                pltpu.VMEM((1, hidden), f32),
                pltpu.VMEM((hidden, hidden), bf16),
                pltpu.VMEM((1, hidden), f32),
                pltpu.VMEM((1, hidden), f32),
                pltpu.VMEM(out_weight.shape, bf16),
                pltpu.VMEM((1, channels), f32),
                pltpu.SemaphoreType.DMA((10,)),
                pltpu.VMEM((4, CH, width), f32),
                pltpu.VMEM((128, hidden), f32),
                pltpu.VMEM((256, hidden), f32),
                pltpu.VMEM((TAPS, hidden), bf16),
                pltpu.VMEM((hidden, TAPS), bf16),
                pltpu.VMEM((TAPS, hidden), bf16),
                pltpu.VMEM((hidden, TAPS), bf16),
                pltpu.VMEM((hidden, hidden), bf16),
                pltpu.VMEM((TAPS, area), bf16),
                pltpu.VMEM((hidden, area), f32),
                pltpu.VMEM((hidden, area), f32),
                pltpu.VMEM((hidden, area), bf16),
                pltpu.VMEM((hidden, area), bf16),
                pltpu.VMEM((hidden, area), bf16),
                pltpu.VMEM((TAPS, area), f32),
                pltpu.VMEM((4 * CH, width), bf16),
                pltpu.VMEM((4 * CH, width), bf16),
                pltpu.VMEM((2 * CH, width), bf16),
                pltpu.VMEM((2 * CH, width), bf16),
                pltpu.VMEM((TERMS, 2, 2 * CH, width), bf16),
                pltpu.VMEM((TERMS, 2, 2 * CH, width), bf16),
                pltpu.VMEM((2, 2 * CH, width), bf16),
                pltpu.VMEM((2, 2 * CH, width), bf16),
                pltpu.VMEM((2, CH, width), bf16),
                pltpu.VMEM((2, CH, width), bf16),
                pltpu.VMEM((2, CH, width), f32),
                pltpu.VMEM((2, CH, width), f32),
                pltpu.VMEM((2, 1, width), f32),
                pltpu.VMEM((2, 1, width), f32),
                pltpu.VMEM((2, width), f32),
                pltpu.VMEM((2, width), f32),
                pltpu.VMEM((1, 128), f32),
                pltpu.VMEM((2, 1, 128), f32),
                pltpu.VMEM((1, 128), f32),
                pltpu.VMEM((n_rows // 2, 1, 128), f32),
                pltpu.SemaphoreType.DMA((TERMS, 2)),
                pltpu.SemaphoreType.DMA((TERMS, 2)),
                pltpu.SemaphoreType.DMA((3, 3)),
                pltpu.SemaphoreType.DMA((3, 3)),
                pltpu.SemaphoreType.DMA((2,)),
                pltpu.SemaphoreType.DMA((2,)),
                pltpu.SemaphoreType.REGULAR((3,)),
            ],
            compiler_params=pltpu.CompilerParams(
                collective_id=0, has_side_effects=True, vmem_limit_bytes=60 * 1024 * 1024
            ),
        )(
            pixels,
            probes,
            in_weight,
            in_bias[None, :],
            in_beta[None, :],
            mid_weight,
            mid_bias[None, :],
            mid_beta[None, :],
            out_weight,
            out_bias[None, :],
        )
        hbm = pl.BlockSpec(memory_space=pltpu.HBM)
        rate = 1.0 / (channels * math.log(2.0) * n_rows * area)
        return pl.pallas_call(
            functools.partial(write_out, rate),
            out_shape=(
                jax.ShapeDtypeStruct(latent.shape, f32),
                jax.ShapeDtypeStruct(bits.shape, f32),
                jax.ShapeDtypeStruct((1,), f32),
            ),
            in_specs=[vmem] * 3,
            out_specs=(hbm, hbm, hbm),
            scratch_shapes=[pltpu.SMEM((1,), f32), pltpu.SemaphoreType.DMA((3,))],
            compiler_params=pltpu.CompilerParams(vmem_limit_bytes=1024 * 1024),
        )(latent, bits, sums)

    placed = (P("batch", "rows", None),) * 2 + (P(),) * 8
    return jax.shard_map(
        per_device,
        mesh=mesh,
        in_specs=placed,
        out_specs=(P("batch", "rows", None), P(("batch", "rows"), None), P("batch")),
        check_vma=False,
    )
```
